256 devices in a mesh: tm: 128 (over x, z, y_hi, core), net: 2 (over y_lo).
Axes of the slice: x: 4, y: 4 (y_hi: 2, y_lo: 2; y = y_hi * 2 + y_lo), z: 8, core: 2. Of those that a mesh axis runs over, the one named last changes fastest.
Arguments:
- jacobian: bfloat16 [524288, 1024], P(('net', 'tm')), parts along dimension 0, may hold values from -24 to 24
- misfit: bfloat16 [524288], P(('net', 'tm')), parts along dimension 0, may hold values from -6 to 6
- taps: float32 [128], P('net'), parts along dimension 0, may hold values from -0.4 to 0.4
Outputs:
- fisher: float32 [2048, 1024], P(('net', 'tm')), parts along dimension 0
- newton: float32 [2048], P(('net', 'tm')), parts along dimension 0
The draws below stay inside these ranges and needn't reach their ends.
There are 2 independent parts, one for each index of `net`. The reference program is written for one: setup_inputs(seed, part) draws one part's arguments, and reference() takes and returns one part's arrays. A program takes and returns all parts, laid end to end along the dimension named above; each array names one. Nothing has to cross between parts.
All inputs are finite; a program needn't handle non-finite values.
Results may differ from the reference program's by a relative error of at most 0.0039.
Values may be sent and summed in bfloat16 or wider, within the bound.
A program may use at most 64 MiB of HBM per device.

```python
import jax
import jax.numpy as jnp

P_SIZE = 1024
ORDER = 64
ROWS_DEV = 2048
TIMES = 262144


def raised(entries, own_key, source, target, shards_of, factor):
    owner, partner = [(jnp.arange(entries.shape[position]) // (entries.shape[position] // shards_of)).reshape([-1 if axis == position else 1 for axis in range(entries.ndim)]) for position in (source, target)]
    chosen = jax.random.permutation(own_key, shards_of)[partner]
    strong = (owner == chosen) | (owner == (partner + shards_of // 2) % shards_of)
    return jnp.where(strong, factor * entries, entries)


def steps_of(key, shape, split, low, top_value):
    level = 1.0
    for dim, parts in split:
        draws = jax.random.uniform(jax.random.fold_in(jax.random.fold_in(key, 6), dim), (parts,), jnp.float32, low / len(split), top_value / len(split))
        level = level * jnp.repeat(jnp.exp(draws), shape[dim] // parts).reshape((-1,) + (1,) * (len(shape) - 1 - dim))
    return level


def gaussian(own_key, shape, scale, most, pieces=(), kind=jnp.bfloat16):
    drawn = scale * jax.random.normal(own_key, shape, jnp.float32)
    if pieces:
        drawn = drawn * steps_of(own_key, shape, pieces, -0.22, 0.18)
    return jnp.clip(drawn, -most, most).astype(kind)


def gaussian_with(stream_key, shape, width, limit, split, heavy, kind=jnp.bfloat16):
    array = width * jax.random.normal(stream_key, shape, jnp.float32)
    if split:
        array = array * steps_of(stream_key, shape, split, -0.22, 0.18)
    return jnp.clip(raised(array, jax.random.fold_in(stream_key, 3), *heavy), -limit, limit).astype(kind)


def setup_inputs(seed: int = 0, part: int = 0) -> dict:
    seeds = jax.random.split(jax.random.key(seed), 4)
    own_keys = jax.random.split(jax.random.fold_in(seeds[3], part), 4)
    jacobian = gaussian_with(own_keys[0], (TIMES, P_SIZE), 1.0, 24.0, ((0, 128),), (0, 1, 128, 5.5))
    misfit = gaussian(own_keys[1], (TIMES,), 1.0, 6.0, ((0, 128),))
    taps = gaussian(own_keys[2], (ORDER,), 0.1, 0.4, (), jnp.float32)
    return {"jacobian": jacobian, "misfit": misfit, "taps": taps}


def tap_matrix(coef, block, order):
    rows = jnp.arange(block, dtype=jnp.int32)[:, None]
    cols = jnp.arange(block + order, dtype=jnp.int32)[None, :]
    lag = rows + order - cols
    lags = jnp.arange(1, order + 1, dtype=jnp.int32)
    picked = jnp.sum(jnp.where(lag[:, :, None] == lags[None, None, :], coef[None, None, :], 0.0), axis=2)
    return jnp.where(lag == 0, 1.0, -picked)


def reference(jacobian, misfit, taps):
    block = min(128, ROWS_DEV)
    count = TIMES // block
    coef = taps.astype(jnp.bfloat16).astype(jnp.float32)
    matrix = tap_matrix(coef, block, ORDER).astype(jnp.bfloat16).astype(jnp.float32)
    jac_blocks = jacobian.reshape(count, block, P_SIZE)
    prev = jnp.concatenate([jnp.zeros((1, ORDER, P_SIZE), jnp.bfloat16), jac_blocks[:-1, block - ORDER:]], axis=0)
    whitened = jnp.einsum("ij,bjp->bip", matrix[:, :ORDER], prev.astype(jnp.float32))
    whitened = whitened + jnp.einsum("ij,bjp->bip", matrix[:, ORDER:], jac_blocks.astype(jnp.float32))
    whitened = whitened.astype(jnp.bfloat16).reshape(TIMES, P_SIZE)
    mis_blocks = misfit.reshape(count, block)
    mis_prev = jnp.concatenate([jnp.zeros((1, ORDER), jnp.bfloat16), mis_blocks[:-1, block - ORDER:]], axis=0)
    white_misfit = jnp.einsum("ij,bj->bi", matrix[:, :ORDER], mis_prev.astype(jnp.float32))
    white_misfit = white_misfit + jnp.einsum("ij,bj->bi", matrix[:, ORDER:], mis_blocks.astype(jnp.float32))
    white_misfit = white_misfit.astype(jnp.bfloat16).reshape(TIMES)
    fisher = jnp.dot(whitened.T, whitened, preferred_element_type=jnp.float32) / TIMES
    gradient = jnp.dot(white_misfit, whitened, preferred_element_type=jnp.float32) / TIMES
    newton = gradient / jnp.diagonal(fisher)
    return fisher, newton
```

```python
import jax
import jax.numpy as jnp
from jax import lax
from jax.experimental import pallas as pl
from jax.experimental.pallas import tpu as pltpu
from jax.sharding import PartitionSpec as P

NX, NZ, NY, NC = 4, 8, 2, 2
NU = NX * NY
OWNERS = NX * NZ * NY * NC
MESH = pl.DeviceIdType.MESH
BF16, F32 = jnp.bfloat16, jnp.float32

ROWS, WIDTH, ORDER = 2048, 1024, 64
BLOCK = 192
CHUNKS = 4
ACOLS = 256
BCOLS = WIDTH - ACOLS
AHALF, BHALF = ACOLS // 2, BCOLS // 2
TOTAL = ROWS * OWNERS
XY_STEPS = [(2, 0), (2, 1), (1, 0), (3, 0), (1, 1), (3, 1), (0, 1)]
Z_STEPS = [4, 3, 5, 2, 6, 1, 7]


def position(x, z, y, c):
    return ((lax.rem(x, NX) * NZ + lax.rem(z, NZ)) * NY + lax.rem(y, NY)) * NC + lax.rem(c, NC)


def folded(rows):
    half = rows.shape[1] // 2
    return jnp.concatenate([rows[:, :half], rows[:, half:]], axis=0)


def unfolded(piece):
    return jnp.concatenate([piece[:8], piece[8:]], axis=1)


def kernel(
    jac, mis, taps, fisher, newton,
    xbuf, white, white_t, wm_rows, mis_tail,
    keep_a, keep_b, core_sa, core_sb, core_ra, core_rb,
    s1a, s1b, r1a, r1b, a2, b2, s2a, s2b, r2a, r2b,
    load_sem, halo_ss, halo_rs, core_ss, core_rs,
    s1a_ss, s1a_rs, s1b_ss, s1b_rs, s2a_ss, s2a_rs, s2b_ss, s2b_rs,
):
    me = lax.axis_index("tm")
    x, z, y, c = me // (NZ * NY * NC), (me // (NY * NC)) % NZ, (me // NC) % NY, me % NC
    sibling = position(x, z, y, c + 1)
    after, before = lax.rem(me + 1, OWNERS), lax.rem(me + OWNERS - 1, OWNERS)
    xy_dev = [position(x + dx, z, y + dy, c) for dx, dy in XY_STEPS]
    xy_own = [lax.rem(x + dx, NX) * NY + lax.rem(y + dy, NY) for dx, dy in XY_STEPS]
    z_dev = [position(x, z + dz, y, c) for dz in Z_STEPS]
    z_own = [lax.rem(z + dz, NZ) for dz in Z_STEPS]
    u = x * NY + y

    step_rows = ROWS // CHUNKS
    loads = []
    for i in reversed(range(CHUNKS)):
        load = pltpu.make_async_copy(
            jac.at[pl.ds(i * step_rows, step_rows)],
            xbuf.at[pl.ds(ORDER + i * step_rows, step_rows)],
            load_sem.at[i],
        )
        load.start()
        loads.append(load)
    loads = loads[::-1]

    barrier = pltpu.get_barrier_semaphore()
    partners = [sibling, after, before] + xy_dev + z_dev
    for device in partners:
        pl.semaphore_signal(barrier, inc=1, device_id={"tm": device}, device_id_type=MESH)

    coef = jnp.broadcast_to(taps[...].astype(BF16), (16, ORDER))
    lag_of = lax.broadcasted_iota(jnp.int32, (ORDER, 256), 0)
    lane_of = lax.broadcasted_iota(jnp.int32, (ORDER, 256), 1)
    flip = (lag_of + lane_of == ORDER - 1).astype(F32).astype(BF16)
    first = jnp.dot(coef, flip, preferred_element_type=F32)[:1]
    lane = lax.broadcasted_iota(jnp.int32, (1, 256), 1)
    first = jnp.where(lane == ORDER, 1.0, -first)
    matrix = pltpu.roll(jnp.broadcast_to(first, (BLOCK, 256)), 0, 1, stride=1, stride_axis=0).astype(BF16)
    mis_matrix = pltpu.roll(jnp.broadcast_to(first, (128, 256)), ORDER, 1, stride=1, stride_axis=0).astype(BF16)

    pl.semaphore_wait(barrier, len(partners))

    halo = pltpu.make_async_remote_copy(
        src_ref=jac.at[pl.ds(ROWS - ORDER, ORDER)], dst_ref=xbuf.at[pl.ds(0, ORDER)],
        send_sem=halo_ss.at[0], recv_sem=halo_rs.at[0], device_id={"tm": after}, device_id_type=MESH,
    )
    mis_halo = pltpu.make_async_remote_copy(
        src_ref=mis, dst_ref=mis_tail,
        send_sem=halo_ss.at[1], recv_sem=halo_rs.at[1], device_id={"tm": after}, device_id_type=MESH,
    )

    @pl.when(me < OWNERS - 1)
    def _():
        halo.start()
        mis_halo.start()

    def whiten(start, rows):
        out = jnp.dot(
            matrix[:rows, : rows + ORDER], xbuf[start : start + rows + ORDER], preferred_element_type=F32
        )
        white[start : start + rows] = out.astype(BF16)

    starts = list(range(0, ROWS, BLOCK))
    ready = CHUNKS
    for start in starts[::-1]:
        rows = min(BLOCK, ROWS - start)
        lowest = max(0, start - ORDER)
        while ready * step_rows > lowest:
            ready -= 1
            loads[ready].wait()
        if start == 0:

            @pl.when(me > 0)
            def _():
                halo.wait_recv()
                mis_halo.wait_recv()

            @pl.when(me == 0)
            def _():
                xbuf[:ORDER] = jnp.zeros((ORDER, WIDTH), BF16)
                mis_tail[...] = jnp.zeros_like(mis_tail)

        whiten(start, rows)

    here = mis[...].astype(F32)
    row_of = lax.broadcasted_iota(jnp.int32, (16, 128), 0)
    previous = jnp.where(
        row_of == 0, pltpu.roll(mis_tail[...].astype(F32), 1, 0), pltpu.roll(here, 1, 0)
    )
    both = jnp.concatenate([previous, here], axis=1).astype(BF16)
    white_mis = lax.dot_general(both, mis_matrix, (((1,), (1,)), ((), ())), preferred_element_type=F32)
    for i in range(16):
        wm_rows[:, i * 128 : (i + 1) * 128] = jnp.broadcast_to(white_mis[i : i + 1], (16, 128)).astype(BF16)

    for i in range(ROWS // 256):
        white_t[:, i * 256 : (i + 1) * 256] = white[i * 256 : (i + 1) * 256].T

    mine_first = c == 0

    def split(rows, grad, owner, offset, keep, send, index):
        pair = []
        for side in range(NC):
            part = rows[side * 8 : side * 8 + 8]
            r = lax.broadcasted_iota(jnp.int32, part.shape, 0)
            col = lax.broadcasted_iota(jnp.int32, part.shape, 1)
            beside = col == (owner + side) * 8 - offset + lax.rem(r + 1, 8)
            pair.append(folded(jnp.where(beside, jnp.broadcast_to(grad, part.shape), part)))
        keep[index] = jnp.where(mine_first, pair[0], pair[1])
        send[index] = jnp.where(mine_first, pair[1], pair[0]).astype(BF16)

    def to_sibling(src, dst, k):
        return pltpu.make_async_remote_copy(
            src_ref=src, dst_ref=dst, send_sem=core_ss.at[k], recv_sem=core_rs.at[k],
            device_id={"tm": sibling}, device_id_type=MESH,
        )

    copies = []
    for xo in range(NX):
        lhs = white_t[xo * 256 : (xo + 1) * 256]
        if xo == 0:
            lhs = jnp.concatenate([lhs, wm_rows[...]], axis=0)
        out = jnp.dot(lhs, white[:, :ACOLS], preferred_element_type=F32)
        if xo == 0:
            grad = out[256:257]
        for zo in range(NZ):
            for yo in range(NY):
                row = (zo * NY + yo) * NC * 8
                split(
                    out[row : row + 16], grad, xo * 32 + (zo * NY + yo) * NC, 0,
                    keep_a, core_sa, zo * NU + xo * NY + yo,
                )
    core_a = to_sibling(core_sa, core_ra, 0)
    core_a.start()
    copies.append(core_a)

    stage1a, stage1b, core_b = [], [], []

    def send_a():
        core_a.wait_recv()
        s1a[...] = (keep_a[...] + core_ra[...].astype(F32)).astype(BF16)
        for k, (device, own) in enumerate(zip(z_dev, z_own)):
            copy = pltpu.make_async_remote_copy(
                src_ref=s1a.at[pl.ds(own * NU, NU)], dst_ref=r1a.at[k],
                send_sem=s1a_ss.at[k], recv_sem=s1a_rs.at[k], device_id={"tm": device}, device_id_type=MESH,
            )
            copy.start()
            stage1a.append(copy)

    def send_b(step):
        dx = X_ORDER[step]
        xo = lax.rem(x + dx, NX)
        core_b[step].wait_recv()
        span = pl.ds(xo * 16, 16)
        s1b[span] = (keep_b[span] + core_rb[span].astype(F32)).astype(BF16)
        for k, (device, own) in enumerate(zip(xy_dev, xy_own)):
            if XY_STEPS[k][0] == dx:
                copy = pltpu.make_async_remote_copy(
                    src_ref=s1b.at[pl.ds(own * NZ, NZ)], dst_ref=r1b.at[k],
                    send_sem=s1b_ss.at[k], recv_sem=s1b_rs.at[k], device_id={"tm": device}, device_id_type=MESH,
                )
                copy.start()
                stage1b.append((k, copy))

    X_ORDER = [2, 1, 3, 0]
    for step, dx in enumerate(X_ORDER):
        xo = lax.rem(x + dx, NX)
        lhs = jnp.concatenate([white_t[pl.ds(pl.multiple_of(xo * 256, 256), 256)], wm_rows[...]], axis=0)
        out = jnp.dot(lhs, white[:, ACOLS:], preferred_element_type=F32)
        grad = out[256:257]
        for zo in range(NZ):
            for yo in range(NY):
                row = (zo * NY + yo) * NC * 8
                split(
                    out[row : row + 16], grad, xo * 32 + (zo * NY + yo) * NC, ACOLS,
                    keep_b, core_sb, (xo * NY + yo) * NZ + zo,
                )
        span = pl.ds(xo * 16, 16)
        copy = to_sibling(core_sb.at[span], core_rb.at[span], 1 + step)
        copy.start()
        core_b.append(copy)
        if step == 0:
            send_a()
        else:
            send_b(step - 1)
    send_b(NX - 1)

    span = pl.ds(z * NU, NU)
    total = keep_a[span] + core_ra[span].astype(F32)
    for k, copy in enumerate(stage1a):
        copy.wait_recv()
        total = total + r1a[k].astype(F32)
    a2[...] = total
    s2a[...] = total.astype(BF16)
    stage2a = []
    for k, (device, own) in enumerate(zip(xy_dev, xy_own)):
        copy = pltpu.make_async_remote_copy(
            src_ref=s2a.at[own], dst_ref=r2a.at[k],
            send_sem=s2a_ss.at[k], recv_sem=s2a_rs.at[k], device_id={"tm": device}, device_id_type=MESH,
        )
        copy.start()
        stage2a.append(copy)

    span = pl.ds(u * NZ, NZ)
    b2[...] = keep_b[span] + core_rb[span].astype(F32)
    for k, copy in stage1b:
        copy.wait_recv()
        b2[...] += r1b[k].astype(F32)
    s2b[...] = b2[...].astype(BF16)
    stage2b = []
    for k, (device, own) in enumerate(zip(z_dev, z_own)):
        copy = pltpu.make_async_remote_copy(
            src_ref=s2b.at[own], dst_ref=r2b.at[k],
            send_sem=s2b_ss.at[k], recv_sem=s2b_rs.at[k], device_id={"tm": device}, device_id_type=MESH,
        )
        copy.start()
        stage2b.append(copy)

    last_a, last_b = a2[u], b2[z]
    for k, copy in enumerate(stage2a):
        copy.wait_recv()
        last_a = last_a + r2a[k].astype(F32)
    for k, copy in enumerate(stage2b):
        copy.wait_recv()
        last_b = last_b + r2b[k].astype(F32)
    rows = jnp.concatenate([unfolded(last_a), unfolded(last_b)], axis=1)

    r = lax.broadcasted_iota(jnp.int32, rows.shape, 0)
    col = lax.broadcasted_iota(jnp.int32, rows.shape, 1) - me * 8
    beside, on = col == lax.rem(r + 1, 8), col == r
    grad = pltpu.roll(jnp.sum(jnp.where(beside, rows, 0.0), axis=1, keepdims=True) + jnp.zeros((8, 128), F32), 1, 0)
    diagonal = jnp.sum(jnp.where(on, rows, 0.0), axis=1, keepdims=True)
    mirrored = jnp.sum(jnp.where(on, pltpu.roll(rows, 7, 0), 0.0), axis=1, keepdims=True)
    fisher[...] = jnp.where(beside, mirrored, rows) * (1.0 / TOTAL)
    ratio = grad / diagonal
    r8 = lax.broadcasted_iota(jnp.int32, (8, 128), 0)
    c8 = lax.broadcasted_iota(jnp.int32, (8, 128), 1)
    newton[...] = jnp.sum(jnp.where(r8 == c8, ratio, 0.0), axis=0, keepdims=True)[:, :8]

    @pl.when(me < OWNERS - 1)
    def _():
        halo.wait_send()
        mis_halo.wait_send()

    for copy in copies + core_b + stage1a + [copy for _, copy in stage1b] + stage2a + stage2b:
        copy.wait_send()


def shards(jacobian, misfit, taps):
    dma = pltpu.SemaphoreType.DMA
    vmem = pl.BlockSpec(memory_space=pltpu.VMEM)
    fisher, newton = pl.pallas_call(
        kernel,
        out_shape=(jax.ShapeDtypeStruct((8, WIDTH), F32), jax.ShapeDtypeStruct((1, 8), F32)),
        in_specs=[pl.BlockSpec(memory_space=pl.ANY), vmem, vmem],
        out_specs=(vmem, vmem),
        scratch_shapes=[
            pltpu.VMEM((ROWS + ORDER, WIDTH), BF16),
            pltpu.VMEM((ROWS, WIDTH), BF16),
            pltpu.VMEM((WIDTH, ROWS), BF16),
            pltpu.VMEM((16, ROWS), BF16),
            pltpu.VMEM((16, 128), BF16),
            pltpu.VMEM((64, 16, AHALF), F32),
            pltpu.VMEM((64, 16, BHALF), F32),
            pltpu.VMEM((64, 16, AHALF), BF16),
            pltpu.VMEM((64, 16, BHALF), BF16),
            pltpu.VMEM((64, 16, AHALF), BF16),
            pltpu.VMEM((64, 16, BHALF), BF16),
            pltpu.VMEM((64, 16, AHALF), BF16),
            pltpu.VMEM((64, 16, BHALF), BF16),
            pltpu.VMEM((7, 8, 16, AHALF), BF16),
            pltpu.VMEM((7, 8, 16, BHALF), BF16),
            pltpu.VMEM((8, 16, AHALF), F32),
            pltpu.VMEM((8, 16, BHALF), F32),
            pltpu.VMEM((8, 16, AHALF), BF16),
            pltpu.VMEM((8, 16, BHALF), BF16),
            pltpu.VMEM((7, 16, AHALF), BF16),
            pltpu.VMEM((7, 16, BHALF), BF16),
            dma((CHUNKS,)), dma((2,)), dma((2,)), dma((5,)), dma((5,)),
            dma((7,)), dma((7,)), dma((7,)), dma((7,)), dma((7,)), dma((7,)), dma((7,)), dma((7,)),
        ],
        compiler_params=pltpu.CompilerParams(
            collective_id=0, has_side_effects=True, vmem_limit_bytes=56 * 1024 * 1024
        ),
    )(jacobian, misfit.reshape(16, 128), taps.reshape(1, ORDER))
    return fisher, newton.reshape(8)


def solution(mesh):
    in_specs = (P(("net", "tm"), None), P(("net", "tm")), P("net"))
    out_specs = (P(("net", "tm"), None), P(("net", "tm")))
    return jax.shard_map(shards, mesh=mesh, in_specs=in_specs, out_specs=out_specs, check_vma=False)
```

```python
import jax
import jax.numpy as jnp
from jax import lax
from jax.experimental import pallas as pl
from jax.experimental.pallas import tpu as pltpu
from jax.sharding import PartitionSpec as P

NX, NZ, NY, NC = 4, 8, 2, 2
NU = NX * NY
OWNERS = NX * NZ * NY * NC
MESH = pl.DeviceIdType.MESH
BF16, F32 = jnp.bfloat16, jnp.float32

ROWS, WIDTH, ORDER = 2048, 1024, 64
BLOCK = 192
CHUNKS = 8
KROWS = 256
ACOLS = 256
BCOLS = WIDTH - ACOLS
AHALF, BHALF = ACOLS // 2, BCOLS // 2
TOTAL = ROWS * OWNERS
XY_STEPS = [(2, 0), (2, 1), (1, 0), (3, 0), (1, 1), (3, 1), (0, 1)]
Z_STEPS = [4, 3, 5, 2, 6, 1, 7]


def position(x, z, y, c):
    return ((lax.rem(x, NX) * NZ + lax.rem(z, NZ)) * NY + lax.rem(y, NY)) * NC + lax.rem(c, NC)


def folded(rows):
    half = rows.shape[1] // 2
    return jnp.concatenate([rows[:, :half], rows[:, half:]], axis=0)


def unfolded(piece):
    return jnp.concatenate([piece[:8], piece[8:]], axis=1)


def beside(base):
    r = lax.broadcasted_iota(jnp.int32, (8, 128), 0)
    lane = lax.broadcasted_iota(jnp.int32, (8, 128), 1) - base
    return lane == lax.rem(r + 1, 8), lane == lax.rem(r + 2, 8)


def two_terms(value):
    high = value.astype(BF16).astype(F32)
    return high, value - high


def place(tile, base, high, low):
    one, two = beside(base)
    return jnp.where(one, high, jnp.where(two, low, tile))


def split_again(tile, base):
    one, two = beside(base)
    high, low = two_terms(jnp.sum(jnp.where(one | two, tile, 0.0), axis=0, keepdims=True))
    return jnp.where(one, high, jnp.where(two, low, tile))


def kernel(
    jac, mis, taps, rows_out,
    xbuf, white, white_t, wm_rows, mis_tail, acc_a, acc_b,
    keep_a, keep_b, core_sa, core_sb, core_ra, core_rb,
    s1a, s1b, r1a, r1b, a2, b2, s2a, s2b, r2a, r2b,
    load_sem, halo_ss, halo_rs, core_ss, core_rs,
    s1a_ss, s1a_rs, s1b_ss, s1b_rs, s2a_ss, s2a_rs, s2b_ss, s2b_rs,
):
    me = lax.axis_index("tm")
    x, z, y, c = me // (NZ * NY * NC), (me // (NY * NC)) % NZ, (me // NC) % NY, me % NC
    sibling = position(x, z, y, c + 1)
    after, before = lax.rem(me + 1, OWNERS), lax.rem(me + OWNERS - 1, OWNERS)
    xy_dev = [position(x + dx, z, y + dy, c) for dx, dy in XY_STEPS]
    xy_own = [lax.rem(x + dx, NX) * NY + lax.rem(y + dy, NY) for dx, dy in XY_STEPS]
    z_dev = [position(x, z + dz, y, c) for dz in Z_STEPS]
    z_own = [lax.rem(z + dz, NZ) for dz in Z_STEPS]
    u = x * NY + y

    step_rows = ROWS // CHUNKS
    loads = []
    for i in reversed(range(CHUNKS)):
        load = pltpu.make_async_copy(
            jac.at[pl.ds(i * step_rows, step_rows)],
            xbuf.at[pl.ds(ORDER + i * step_rows, step_rows)],
            load_sem.at[i],
        )
        load.start()
        loads.append(load)
    loads = loads[::-1]

    barrier = pltpu.get_barrier_semaphore()
    partners = [sibling, after, before] + xy_dev + z_dev
    for device in partners:
        pl.semaphore_signal(barrier, inc=1, device_id={"tm": device}, device_id_type=MESH)

    coef = jnp.broadcast_to(taps[...].astype(BF16), (16, ORDER))
    lag_of = lax.broadcasted_iota(jnp.int32, (ORDER, 256), 0)
    lane_of = lax.broadcasted_iota(jnp.int32, (ORDER, 256), 1)
    flip = (lag_of + lane_of == ORDER - 1).astype(F32).astype(BF16)
    first = jnp.dot(coef, flip, preferred_element_type=F32)[:1]
    lane = lax.broadcasted_iota(jnp.int32, (1, 256), 1)
    first = jnp.where(lane == ORDER, 1.0, -first)
    matrix = pltpu.roll(jnp.broadcast_to(first, (BLOCK, 256)), 0, 1, stride=1, stride_axis=0).astype(BF16)
    mis_matrix = pltpu.roll(jnp.broadcast_to(first, (128, 256)), ORDER, 1, stride=1, stride_axis=0).astype(BF16)

    def whiten_misfit(tail):
        here = mis[...].astype(F32)
        row_of = lax.broadcasted_iota(jnp.int32, (16, 128), 0)
        previous = jnp.where(row_of == 0, pltpu.roll(tail, 1, 0), pltpu.roll(here, 1, 0))
        both = jnp.concatenate([previous, here], axis=1).astype(BF16)
        return lax.dot_general(both, mis_matrix, (((1,), (1,)), ((), ())), preferred_element_type=F32)

    def put_misfit(white_mis, i):
        wm_rows[:, i * 128 : (i + 1) * 128] = jnp.broadcast_to(white_mis[i : i + 1], (16, 128)).astype(BF16)

    white_mis = whiten_misfit(jnp.zeros((16, 128), F32))
    for i in range(1, 16):
        put_misfit(white_mis, i)

    def whiten(start, rows):
        out = jnp.dot(
            matrix[:rows, : rows + ORDER], xbuf[start : start + rows + ORDER], preferred_element_type=F32
        )
        white[start : start + rows] = out.astype(BF16)

    def transpose(i):
        white_t[:, i * KROWS : (i + 1) * KROWS] = white[i * KROWS : (i + 1) * KROWS].T

    ready, turned = CHUNKS, ROWS // KROWS
    for start in list(range(0, ROWS, BLOCK))[:0:-1]:
        rows = min(BLOCK, ROWS - start)
        while ready * step_rows > start - ORDER:
            ready -= 1
            loads[ready].wait()
        whiten(start, rows)
        while (turned - 1) * KROWS >= start:
            turned -= 1
            transpose(turned)
    while ready > 0:
        ready -= 1
        loads[ready].wait()

    pl.semaphore_wait(barrier, len(partners))

    halo = pltpu.make_async_remote_copy(
        src_ref=jac.at[pl.ds(ROWS - ORDER, ORDER)], dst_ref=xbuf.at[pl.ds(0, ORDER)],
        send_sem=halo_ss.at[0], recv_sem=halo_rs.at[0], device_id={"tm": after}, device_id_type=MESH,
    )
    mis_halo = pltpu.make_async_remote_copy(
        src_ref=mis, dst_ref=mis_tail,
        send_sem=halo_ss.at[1], recv_sem=halo_rs.at[1], device_id={"tm": after}, device_id_type=MESH,
    )

    @pl.when(me < OWNERS - 1)
    def _():
        halo.start()
        mis_halo.start()

    def gram_a(low, high):
        lhs = jnp.concatenate([white_t[:, low:high], wm_rows[:, low:high]], axis=0)
        return jnp.dot(lhs, white[low:high, :ACOLS], preferred_element_type=F32)

    def gram_b(xo, low, high):
        lhs = white_t[pl.ds(pl.multiple_of(xo * 256, 256), 256), low:high]
        lhs = jnp.concatenate([lhs, wm_rows[:, low:high]], axis=0)
        return jnp.dot(lhs, white[low:high, ACOLS:], preferred_element_type=F32)

    x_order = [2, 1, 3, 0]
    x_of = [lax.rem(x + dx, NX) for dx in x_order]

    acc_a[...] = gram_a(KROWS, ROWS)
    acc_b[0] = gram_b(x_of[0], KROWS, ROWS)

    @pl.when(me > 0)
    def _():
        halo.wait_recv()
        mis_halo.wait_recv()

    @pl.when(me == 0)
    def _():
        xbuf[:ORDER] = jnp.zeros((ORDER, WIDTH), BF16)
        mis_tail[...] = jnp.zeros_like(mis_tail)

    whiten(0, BLOCK)
    transpose(0)
    put_misfit(whiten_misfit(mis_tail[...].astype(F32)), 0)

    def to_sibling(src, dst, k):
        return pltpu.make_async_remote_copy(
            src_ref=src, dst_ref=dst, send_sem=core_ss.at[k], recv_sem=core_rs.at[k],
            device_id={"tm": sibling}, device_id_type=MESH,
        )

    def deal(take, row, keep, send, index):
        keep[index] = folded(take(row + 8 * c))
        send[index] = folded(take(row + 8 - 8 * c)).astype(BF16)

    def eight(row):
        return pl.ds(pl.multiple_of(row, 8), 8)

    acc_a[...] += gram_a(0, KROWS)
    terms = [two_terms(acc_a[WIDTH : WIDTH + 8, t * 128 : t * 128 + 128]) for t in range(2)]
    for own in range(NZ * NY * NC):
        t = own // 16
        at = (slice(own * 8, own * 8 + 8), slice(t * 128, t * 128 + 128))
        acc_a[at] = place(acc_a[at], own % 16 * 8, *terms[t])
    for xo in range(NX):
        for zo in range(NZ):
            for yo in range(NY):
                row = xo * 256 + (zo * NY + yo) * NC * 8
                deal(lambda row: acc_a[eight(row)], row, keep_a, core_sa, zo * NU + xo * NY + yo)
    core_a = to_sibling(core_sa, core_ra, 0)
    core_a.start()

    stage1a, stage1b, core_b = [], [], []

    def tile_of(xo, high):
        return jnp.maximum(xo * 2 + high - 2, 0), jnp.where(xo > 0, 0, 4096)

    def finish_b(step):
        xo = x_of[step]
        for high in range(2):
            tile, off = tile_of(xo, high)
            lanes = pl.ds(pl.multiple_of(tile * 128, 128), 128)
            high_term, low_term = two_terms(acc_b[step, 256:264, lanes])
            for own in range(16):
                row = high * 128 + own * 8
                acc_b[step, row : row + 8, lanes] = place(
                    acc_b[step, row : row + 8, lanes], own * 8 + off, high_term, low_term
                )
        for zo in range(NZ):
            for yo in range(NY):
                deal(
                    lambda row: acc_b[step, eight(row)], (zo * NY + yo) * NC * 8,
                    keep_b, core_sb, (xo * NY + yo) * NZ + zo,
                )
        span = pl.ds(xo * 16, 16)
        copy = to_sibling(core_sb.at[span], core_rb.at[span], 1 + step)
        copy.start()
        core_b.append(copy)

    def again_b(ref, index, xo, high, base):
        tile, off = tile_of(xo, high)
        at = (index, eight(tile // 3 * 8), pl.ds(pl.multiple_of(tile % 3 * 128, 128), 128))
        ref[at] = split_again(ref[at], base + off)

    def send_a():
        core_a.wait_recv()
        keep_a[...] += core_ra[...].astype(F32)
        for zo in range(NZ):
            for yo in range(NY):
                at = (zo * NU + yo, slice(zo // 4 * 8, zo // 4 * 8 + 8))
                keep_a[at] = split_again(keep_a[at], (zo % 4 * 4 + yo * NC + c) * 8)
        s1a[...] = keep_a[...].astype(BF16)
        for k, (device, own) in enumerate(zip(z_dev, z_own)):
            copy = pltpu.make_async_remote_copy(
                src_ref=s1a.at[pl.ds(own * NU, NU)], dst_ref=r1a.at[k],
                send_sem=s1a_ss.at[k], recv_sem=s1a_rs.at[k], device_id={"tm": device}, device_id_type=MESH,
            )
            copy.start()
            stage1a.append(copy)

    def send_b(step):
        xo = x_of[step]
        core_b[step].wait_recv()
        span = pl.ds(xo * 16, 16)
        keep_b[span] += core_rb[span].astype(F32)
        for yo in range(NY):
            for zo in range(NZ):
                again_b(keep_b, (xo * NY + yo) * NZ + zo, xo, zo // 4, (zo % 4 * 4 + yo * NC + c) * 8)
        s1b[span] = keep_b[span].astype(BF16)
        for k, (device, own) in enumerate(zip(xy_dev, xy_own)):
            if XY_STEPS[k][0] == x_order[step]:
                copy = pltpu.make_async_remote_copy(
                    src_ref=s1b.at[pl.ds(own * NZ, NZ)], dst_ref=r1b.at[k],
                    send_sem=s1b_ss.at[k], recv_sem=s1b_rs.at[k], device_id={"tm": device}, device_id_type=MESH,
                )
                copy.start()
                stage1b.append((k, copy))

    acc_b[0] += gram_b(x_of[0], 0, KROWS)
    finish_b(0)
    for step in range(1, NX):
        acc_b[step] = gram_b(x_of[step], 0, ROWS)
        finish_b(step)
        if step == 1:
            send_a()
        send_b(step - 1)
    send_b(NX - 1)

    a2[...] = keep_a[pl.ds(z * NU, NU)]
    for k, copy in enumerate(stage1a):
        copy.wait_recv()
        a2[...] += r1a[k].astype(F32)
    for yo in range(NY):
        at = (yo, eight(z // 4 * 8))
        a2[at] = split_again(a2[at], (z % 4 * 4 + yo * NC + c) * 8)
    s2a[...] = a2[...].astype(BF16)
    stage2a = []
    for k, (device, own) in enumerate(zip(xy_dev, xy_own)):
        copy = pltpu.make_async_remote_copy(
            src_ref=s2a.at[own], dst_ref=r2a.at[k],
            send_sem=s2a_ss.at[k], recv_sem=s2a_rs.at[k], device_id={"tm": device}, device_id_type=MESH,
        )
        copy.start()
        stage2a.append(copy)

    b2[...] = keep_b[pl.ds(u * NZ, NZ)]
    for k, copy in stage1b:
        copy.wait_recv()
        b2[...] += r1b[k].astype(F32)
    for zo in range(NZ):
        again_b(b2, zo, x, zo // 4, (zo % 4 * 4 + y * NC + c) * 8)
    s2b[...] = b2[...].astype(BF16)
    stage2b = []
    for k, (device, own) in enumerate(zip(z_dev, z_own)):
        copy = pltpu.make_async_remote_copy(
            src_ref=s2b.at[own], dst_ref=r2b.at[k],
            send_sem=s2b_ss.at[k], recv_sem=s2b_rs.at[k], device_id={"tm": device}, device_id_type=MESH,
        )
        copy.start()
        stage2b.append(copy)

    last_a, last_b = a2[u], b2[z]
    for k, copy in enumerate(stage2a):
        copy.wait_recv()
        last_a = last_a + r2a[k].astype(F32)

    @pl.when(me < OWNERS - 1)
    def _():
        halo.wait_send()
        mis_halo.wait_send()

    for copy in [core_a] + core_b + stage1a + [copy for _, copy in stage1b] + stage2a:
        copy.wait_send()

    for k, copy in enumerate(stage2b):
        copy.wait_recv()
        last_b = last_b + r2b[k].astype(F32)
    rows_out[:, :ACOLS] = unfolded(last_a)
    rows_out[:, ACOLS:] = unfolded(last_b)

    for copy in stage2b:
        copy.wait_send()


def outputs(rows_ref, fisher, newton):
    rows = rows_ref[...]
    r = lax.broadcasted_iota(jnp.int32, rows.shape, 0)
    col = lax.broadcasted_iota(jnp.int32, rows.shape, 1) - lax.axis_index("tm") * 8
    one, two, on = col == lax.rem(r + 1, 8), col == lax.rem(r + 2, 8), col == r

    def picked(mask, values):
        return jnp.broadcast_to(jnp.sum(jnp.where(mask, values, 0.0), axis=1, keepdims=True), (8, 128))

    grad = pltpu.roll(picked(one, rows), 1, 0) + pltpu.roll(picked(two, rows), 2, 0)
    diagonal = picked(on, rows)
    mirror_one = picked(on, pltpu.roll(rows, 7, 0))[:, :1]
    mirror_two = picked(on, pltpu.roll(rows, 6, 0))[:, :1]
    fisher[...] = jnp.where(one, mirror_one, jnp.where(two, mirror_two, rows)) * (1.0 / TOTAL)
    r8 = lax.broadcasted_iota(jnp.int32, (8, 128), 0)
    c8 = lax.broadcasted_iota(jnp.int32, (8, 128), 1)
    newton[...] = jnp.sum(jnp.where(r8 == c8, grad / diagonal, 0.0), axis=0, keepdims=True)[:, :8]


def shards(jacobian, misfit, taps):
    dma = pltpu.SemaphoreType.DMA
    vmem = pl.BlockSpec(memory_space=pltpu.VMEM)
    rows = pl.pallas_call(
        kernel,
        out_shape=jax.ShapeDtypeStruct((8, WIDTH), F32),
        in_specs=[pl.BlockSpec(memory_space=pl.ANY), vmem, vmem],
        out_specs=vmem,
        scratch_shapes=[
            pltpu.VMEM((ROWS + ORDER, WIDTH), BF16),
            pltpu.VMEM((ROWS, WIDTH), BF16),
            pltpu.VMEM((WIDTH, ROWS), BF16),
            pltpu.VMEM((16, ROWS), BF16),
            pltpu.VMEM((16, 128), BF16),
            pltpu.VMEM((WIDTH + 16, ACOLS), F32),
            pltpu.VMEM((NX, 256 + 16, BCOLS), F32),
            pltpu.VMEM((64, 16, AHALF), F32),
            pltpu.VMEM((64, 16, BHALF), F32),
            pltpu.VMEM((64, 16, AHALF), BF16),
            pltpu.VMEM((64, 16, BHALF), BF16),
            pltpu.VMEM((64, 16, AHALF), BF16),
            pltpu.VMEM((64, 16, BHALF), BF16),
            pltpu.VMEM((64, 16, AHALF), BF16),
            pltpu.VMEM((64, 16, BHALF), BF16),
            pltpu.VMEM((7, 8, 16, AHALF), BF16),
            pltpu.VMEM((7, 8, 16, BHALF), BF16),
            pltpu.VMEM((8, 16, AHALF), F32),
            pltpu.VMEM((8, 16, BHALF), F32),
            pltpu.VMEM((8, 16, AHALF), BF16),
            pltpu.VMEM((8, 16, BHALF), BF16),
            pltpu.VMEM((7, 16, AHALF), BF16),
            pltpu.VMEM((7, 16, BHALF), BF16),
            dma((CHUNKS,)), dma((2,)), dma((2,)), dma((5,)), dma((5,)),
            dma((7,)), dma((7,)), dma((7,)), dma((7,)), dma((7,)), dma((7,)), dma((7,)), dma((7,)),
        ],
        compiler_params=pltpu.CompilerParams(
            collective_id=0, has_side_effects=True, vmem_limit_bytes=56 * 1024 * 1024
        ),
    )(jacobian, misfit.reshape(16, 128), taps.reshape(1, ORDER))
    fisher, newton = pl.pallas_call(
        outputs,
        out_shape=(jax.ShapeDtypeStruct((8, WIDTH), F32), jax.ShapeDtypeStruct((1, 8), F32)),
        in_specs=[vmem],
        out_specs=(vmem, vmem),
    )(rows)
    return fisher, newton.reshape(8)


def solution(mesh):
    in_specs = (P(("net", "tm"), None), P(("net", "tm")), P("net"))
    out_specs = (P(("net", "tm"), None), P(("net", "tm")))
    return jax.shard_map(shards, mesh=mesh, in_specs=in_specs, out_specs=out_specs, check_vma=False)
```

```python
import jax
import jax.numpy as jnp
from jax import lax
from jax.experimental import pallas as pl
from jax.experimental.pallas import tpu as pltpu
from jax.sharding import PartitionSpec as P

NX, NZ, NY, NC = 4, 8, 2, 2
NU = NX * NY
OWNERS = NX * NZ * NY * NC
MESH = pl.DeviceIdType.MESH
BF16, F32 = jnp.bfloat16, jnp.float32

ROWS, WIDTH, ORDER = 2048, 1024, 64
BLOCK = 192
GREET = 4
CHUNKS = 8
KROWS = 256
ACOLS = 256
BCOLS = WIDTH - ACOLS
AHALF, BHALF = ACOLS // 2, BCOLS // 2
TOTAL = ROWS * OWNERS
XY_STEPS = [(2, 0), (2, 1), (1, 0), (3, 0), (1, 1), (3, 1), (0, 1)]
Z_STEPS = [4, 3, 5, 2, 6, 1, 7]
HALVES, NP = 2, NZ // 2


def position(x, z, y, c):
    return ((lax.rem(x, NX) * NZ + lax.rem(z, NZ)) * NY + lax.rem(y, NY)) * NC + lax.rem(c, NC)


def folded(rows):
    half = rows.shape[1] // 2
    return jnp.concatenate([rows[:, :half], rows[:, half:]], axis=0)


def unfolded(piece):
    return jnp.concatenate([piece[:8], piece[8:]], axis=1)


def place_of(step):
    return (step - 2) % NZ


def beside(shape, base):
    r = lax.broadcasted_iota(jnp.int32, shape, 0)
    lane = lax.broadcasted_iota(jnp.int32, shape, 1) - base
    return lane == lax.rem(r + 1, 8), lane == lax.rem(r + 2, 8)


def two_terms(value):
    high = value.astype(BF16).astype(F32)
    return high, value - high


def place(rows, base, grad):
    one, two = beside(rows.shape, base)
    high, low = two_terms(grad)
    return jnp.where(one, high, jnp.where(two, low, rows))


def split_again(rows, base):
    one, two = beside(rows.shape, base)
    high, low = two_terms(jnp.sum(jnp.where(one | two, rows, 0.0), axis=0, keepdims=True))
    return jnp.where(one, high, jnp.where(two, low, rows))


def in_tiles(rows, first, change):
    if first < 0 or first * 128 >= rows.shape[1]:
        return rows
    low, high = first * 128, first * 128 + 256
    parts = [rows[:, :low], change(rows[:, low:high]), rows[:, high:]]
    return jnp.concatenate([part for part in parts if part.shape[1]], axis=1)


def kernel(
    jac, mis, taps, rows_out,
    xbuf, white, white_t, wm_rows, mis_tail, acc,
    keep_a, keep_b, core_sa, core_sb, core_ra, core_rb,
    s1a, s1b, r1a, r1b, a2, b2, s2a, s2b, r2a, r2b,
    load_sem, halo_ss, halo_rs, core_ss, core_rs,
    s1a_ss, s1a_rs, s1b_ss, s1b_rs, s2a_ss, s2a_rs, s2b_ss, s2b_rs,
):
    me = lax.axis_index("tm")
    x, z, y, c = me // (NZ * NY * NC), (me // (NY * NC)) % NZ, (me // NC) % NY, me % NC
    sibling = position(x, z, y, c + 1)
    after, before = lax.rem(me + 1, OWNERS), lax.rem(me + OWNERS - 1, OWNERS)
    xy_dev = [position(x + dx, z, y + dy, c) for dx, dy in XY_STEPS]
    xy_own = [lax.rem(x + dx, NX) * NY + lax.rem(y + dy, NY) for dx, dy in XY_STEPS]
    z_dev = [position(x, z + dz, y, c) for dz in Z_STEPS]
    z_own = [lax.rem(z + dz, NZ) for dz in Z_STEPS]
    u = x * NY + y
    z_place = [lax.rem(zo + 2 * NZ - z - 2, NZ) for zo in range(NZ)]
    z_rows = [p // NP * 512 + p % NP * 32 for p in z_place]
    z_at = [lax.rem(z + 2 + p, NZ) for p in range(NZ)]

    step_rows = ROWS // CHUNKS
    loads = []
    for i in reversed(range(CHUNKS)):
        load = pltpu.make_async_copy(
            jac.at[pl.ds(i * step_rows, step_rows)],
            xbuf.at[pl.ds(ORDER + i * step_rows, step_rows)],
            load_sem.at[i],
        )
        load.start()
        loads.append(load)
    loads = loads[::-1]

    barrier = pltpu.get_barrier_semaphore()
    partners = [sibling, after, before] + xy_dev + z_dev
    for device in partners:
        pl.semaphore_signal(barrier, inc=1, device_id={"tm": device}, device_id_type=MESH)

    coef = jnp.broadcast_to(taps[...].astype(BF16), (16, ORDER))
    lag_of = lax.broadcasted_iota(jnp.int32, (ORDER, 256), 0)
    lane_of = lax.broadcasted_iota(jnp.int32, (ORDER, 256), 1)
    flip = (lag_of + lane_of == ORDER - 1).astype(F32).astype(BF16)
    first = jnp.dot(coef, flip, preferred_element_type=F32)[:1]
    lane = lax.broadcasted_iota(jnp.int32, (1, 256), 1)
    first = jnp.where(lane == ORDER, 1.0, -first)
    matrix = pltpu.roll(jnp.broadcast_to(first, (BLOCK, 256)), 0, 1, stride=1, stride_axis=0).astype(BF16)
    mis_matrix = pltpu.roll(jnp.broadcast_to(first, (128, 256)), ORDER, 1, stride=1, stride_axis=0).astype(BF16)

    def whiten_misfit(tail):
        here = mis[...].astype(F32)
        row_of = lax.broadcasted_iota(jnp.int32, (16, 128), 0)
        previous = jnp.where(row_of == 0, pltpu.roll(tail, 1, 0), pltpu.roll(here, 1, 0))
        both = jnp.concatenate([previous, here], axis=1).astype(BF16)
        return lax.dot_general(both, mis_matrix, (((1,), (1,)), ((), ())), preferred_element_type=F32)

    def put_misfit(white_mis, i):
        wm_rows[:, i * 128 : (i + 1) * 128] = jnp.broadcast_to(white_mis[i : i + 1], (16, 128)).astype(BF16)

    white_mis = whiten_misfit(jnp.zeros((16, 128), F32))
    for i in range(1, 16):
        put_misfit(white_mis, i)

    def whiten(start, rows):
        out = jnp.dot(
            matrix[:rows, : rows + ORDER], xbuf[start : start + rows + ORDER], preferred_element_type=F32
        )
        white[start : start + rows] = out.astype(BF16)

    def transpose(i):
        block = white[i * KROWS : (i + 1) * KROWS].T
        for zo in range(NZ):
            for xo in range(NX):
                rows = pl.ds(pl.multiple_of(z_rows[zo] + xo * 128, 32), 32)
                white_t[rows, i * KROWS : (i + 1) * KROWS] = block[xo * 256 + zo * 32 : xo * 256 + zo * 32 + 32]

    halo = pltpu.make_async_remote_copy(
        src_ref=jac.at[pl.ds(ROWS - ORDER, ORDER)], dst_ref=xbuf.at[pl.ds(0, ORDER)],
        send_sem=halo_ss.at[0], recv_sem=halo_rs.at[0], device_id={"tm": after}, device_id_type=MESH,
    )
    mis_halo = pltpu.make_async_remote_copy(
        src_ref=mis, dst_ref=mis_tail,
        send_sem=halo_ss.at[1], recv_sem=halo_rs.at[1], device_id={"tm": after}, device_id_type=MESH,
    )

    ready, turned = CHUNKS, ROWS // KROWS
    for start in list(range(0, ROWS, BLOCK))[:0:-1]:
        rows = min(BLOCK, ROWS - start)
        while ready * step_rows > start - ORDER:
            ready -= 1
            loads[ready].wait()
        if start == GREET * BLOCK:
            pl.semaphore_wait(barrier, len(partners))

            @pl.when(me < OWNERS - 1)
            def _():
                halo.start()
                mis_halo.start()

        whiten(start, rows)
        while (turned - 1) * KROWS >= start:
            turned -= 1
            transpose(turned)
    while ready > 0:
        ready -= 1
        loads[ready].wait()

    def gram_a(low, high):
        lhs = jnp.concatenate([white_t[:, low:high], wm_rows[:, low:high]], axis=0)
        return jnp.dot(lhs, white[low:high, :ACOLS], preferred_element_type=F32)

    def gram_b(half, low, high):
        lhs = white_t[half * 512 : half * 512 + 512, low:high]
        lhs = jnp.concatenate([lhs, wm_rows[:, low:high]], axis=0)
        return jnp.dot(lhs, white[low:high, ACOLS:], preferred_element_type=F32)

    acc[...] = gram_b(0, KROWS, ROWS)

    @pl.when(me > 0)
    def _():
        halo.wait_recv()
        mis_halo.wait_recv()

    @pl.when(me == 0)
    def _():
        xbuf[:ORDER] = jnp.zeros((ORDER, WIDTH), BF16)
        mis_tail[...] = jnp.zeros_like(mis_tail)

    whiten(0, BLOCK)
    transpose(0)
    put_misfit(whiten_misfit(mis_tail[...].astype(F32)), 0)

    def to_sibling(src, dst, k):
        return pltpu.make_async_remote_copy(
            src_ref=src, dst_ref=dst, send_sem=core_ss.at[k], recv_sem=core_rs.at[k],
            device_id={"tm": sibling}, device_id_type=MESH,
        )

    mine_first = c == 0

    def base_of(p, yo, side):
        return z_at[p] * 32 + (yo * NC + side) * 8

    def deal(rows, grad, first, p, yo, keep, send, index):
        pair = []
        for side in range(NC):
            part = rows[side * 8 : side * 8 + 8]

            def change(tiles, side=side):
                return place(tiles, base_of(p, yo, side), grad[:, first * 128 : first * 128 + 256])

            pair.append(folded(in_tiles(part, first, change)))
        keep[index] = jnp.where(mine_first, pair[0], pair[1])
        send[index] = jnp.where(mine_first, pair[1], pair[0]).astype(BF16)

    def both_cores(keep, received, index, first, p, yo):
        rows = keep[index] + received[index].astype(F32)
        if first < 0 or first * 128 >= 2 * rows.shape[1]:
            return rows.astype(BF16)
        rows = in_tiles(unfolded(rows), first, lambda tiles: split_again(tiles, base_of(p, yo, c)))
        return folded(rows).astype(BF16)

    stage1a, stage1b, core_b = [], [], []

    def finish_b(half, out):
        for xo in range(NX):
            for pp in range(NP):
                for yo in range(NY):
                    row = xo * 128 + pp * 32 + yo * 16
                    deal(
                        out[row : row + 16], out[512:513], xo * 2 - 2, half * NP + pp, yo,
                        keep_b, core_sb, (half * NU + xo * NY + yo) * NP + pp,
                    )
        span = pl.ds(half * NU * NP, NU * NP)
        copy = to_sibling(core_sb.at[span], core_rb.at[span], 1 + half)
        copy.start()
        core_b.append(copy)

    def send_b(half):
        core_b[half].wait_recv()
        for xo in range(NX):
            for yo in range(NY):
                for pp in range(NP):
                    index = (half * NU + xo * NY + yo) * NP + pp
                    s1b[index] = both_cores(keep_b, core_rb, index, xo * 2 - 2, half * NP + pp, yo)
        for k, (device, own) in enumerate(zip(xy_dev, xy_own)):
            copy = pltpu.make_async_remote_copy(
                src_ref=s1b.at[pl.ds((half * NU + own) * NP, NP)], dst_ref=r1b.at[half, k],
                send_sem=s1b_ss.at[half * 7 + k], recv_sem=s1b_rs.at[half * 7 + k],
                device_id={"tm": device}, device_id_type=MESH,
            )
            copy.start()
            stage1b.append(copy)

    finish_b(0, acc[...] + gram_b(0, 0, KROWS))

    out = gram_a(0, ROWS)
    for half in range(HALVES):
        for xo in range(NX):
            for pp in range(NP):
                for yo in range(NY):
                    row = half * 512 + xo * 128 + pp * 32 + yo * 16
                    p = half * NP + pp
                    deal(
                        out[row : row + 16], out[WIDTH : WIDTH + 1], xo * 2, p, yo,
                        keep_a, core_sa, p * NU + xo * NY + yo,
                    )
    core_a = to_sibling(core_sa, core_ra, 0)
    core_a.start()
    send_b(0)

    finish_b(1, gram_b(1, 0, ROWS))

    core_a.wait_recv()
    for p in range(NZ):
        for xo in range(NX):
            for yo in range(NY):
                index = p * NU + xo * NY + yo
                s1a[index] = both_cores(keep_a, core_ra, index, xo * 2, p, yo)
    for k, (device, step) in enumerate(zip(z_dev, Z_STEPS)):
        copy = pltpu.make_async_remote_copy(
            src_ref=s1a.at[pl.ds(place_of(step) * NU, NU)], dst_ref=r1a.at[k],
            send_sem=s1a_ss.at[k], recv_sem=s1a_rs.at[k], device_id={"tm": device}, device_id_type=MESH,
        )
        copy.start()
        stage1a.append(copy)
    send_b(1)

    stage2b = {}

    def pass_b(half):
        span = pl.ds((half * NU + u) * NP, NP)
        b2[half] = keep_b[span] + core_rb[span].astype(F32)
        for k in range(7):
            stage1b[half * 7 + k].wait_recv()
            b2[half] += r1b[half, k].astype(F32)
        for pp in range(NP):
            p = half * NP + pp
            lane = x * 256 - ACOLS + base_of(p, y, c)
            s2b[p] = folded(split_again(unfolded(b2[half, pp]), lane)).astype(BF16)
        for k, (device, step) in enumerate(zip(z_dev, Z_STEPS)):
            p = place_of(step)
            if p // NP == half:
                copy = pltpu.make_async_remote_copy(
                    src_ref=s2b.at[p], dst_ref=r2b.at[k],
                    send_sem=s2b_ss.at[k], recv_sem=s2b_rs.at[k], device_id={"tm": device}, device_id_type=MESH,
                )
                copy.start()
                stage2b[k] = copy

    pass_b(0)

    span = pl.ds(place_of(0) * NU, NU)
    a2[...] = keep_a[span] + core_ra[span].astype(F32)
    for k, copy in enumerate(stage1a):
        copy.wait_recv()
        a2[...] += r1a[k].astype(F32)
    for xo in range(NX):
        for yo in range(NY):
            rows = a2[xo * NY + yo]
            if xo == 0:
                rows = folded(split_again(unfolded(rows), base_of(place_of(0), yo, c)))
            s2a[xo * NY + yo] = rows.astype(BF16)
    stage2a = []
    for k, (device, own) in enumerate(zip(xy_dev, xy_own)):
        copy = pltpu.make_async_remote_copy(
            src_ref=s2a.at[own], dst_ref=r2a.at[k],
            send_sem=s2a_ss.at[k], recv_sem=s2a_rs.at[k], device_id={"tm": device}, device_id_type=MESH,
        )
        copy.start()
        stage2a.append(copy)

    pass_b(1)

    last_a, last_b = a2[u], b2[place_of(0) // NP, place_of(0) % NP]
    for k, copy in enumerate(stage2a):
        copy.wait_recv()
        last_a = last_a + r2a[k].astype(F32)

    @pl.when(me < OWNERS - 1)
    def _():
        halo.wait_send()
        mis_halo.wait_send()

    for copy in [core_a] + core_b + stage1a + stage1b + stage2a:
        copy.wait_send()

    for k, copy in stage2b.items():
        copy.wait_recv()
        last_b = last_b + r2b[k].astype(F32)
    rows_out[:, :ACOLS] = unfolded(last_a)
    rows_out[:, ACOLS:] = unfolded(last_b)

    for copy in stage2b.values():
        copy.wait_send()


def outputs(rows_ref, fisher, newton):
    rows = rows_ref[...]
    r = lax.broadcasted_iota(jnp.int32, rows.shape, 0)
    col = lax.broadcasted_iota(jnp.int32, rows.shape, 1) - lax.axis_index("tm") * 8
    one, two, on = col == lax.rem(r + 1, 8), col == lax.rem(r + 2, 8), col == r

    def picked(mask, values):
        return jnp.broadcast_to(jnp.sum(jnp.where(mask, values, 0.0), axis=1, keepdims=True), (8, 128))

    grad = pltpu.roll(picked(one, rows), 1, 0) + pltpu.roll(picked(two, rows), 2, 0)
    diagonal = picked(on, rows)
    mirror_one = picked(on, pltpu.roll(rows, 7, 0))[:, :1]
    mirror_two = picked(on, pltpu.roll(rows, 6, 0))[:, :1]
    fisher[...] = jnp.where(one, mirror_one, jnp.where(two, mirror_two, rows)) * (1.0 / TOTAL)
    r8 = lax.broadcasted_iota(jnp.int32, (8, 128), 0)
    c8 = lax.broadcasted_iota(jnp.int32, (8, 128), 1)
    newton[...] = jnp.sum(jnp.where(r8 == c8, grad / diagonal, 0.0), axis=0, keepdims=True)[:, :8]


def shards(jacobian, misfit, taps):
    dma = pltpu.SemaphoreType.DMA
    vmem = pl.BlockSpec(memory_space=pltpu.VMEM)
    rows = pl.pallas_call(
        kernel,
        out_shape=jax.ShapeDtypeStruct((8, WIDTH), F32),
        in_specs=[pl.BlockSpec(memory_space=pl.ANY), vmem, vmem],
        out_specs=vmem,
        scratch_shapes=[
            pltpu.VMEM((ROWS + ORDER, WIDTH), BF16),
            pltpu.VMEM((ROWS, WIDTH), BF16),
            pltpu.VMEM((WIDTH, ROWS), BF16),
            pltpu.VMEM((16, ROWS), BF16),
            pltpu.VMEM((16, 128), BF16),
            pltpu.VMEM((512 + 16, BCOLS), F32),
            pltpu.VMEM((64, 16, AHALF), F32),
            pltpu.VMEM((64, 16, BHALF), F32),
            pltpu.VMEM((64, 16, AHALF), BF16),
            pltpu.VMEM((64, 16, BHALF), BF16),
            pltpu.VMEM((64, 16, AHALF), BF16),
            pltpu.VMEM((64, 16, BHALF), BF16),
            pltpu.VMEM((64, 16, AHALF), BF16),
            pltpu.VMEM((64, 16, BHALF), BF16),
            pltpu.VMEM((7, 8, 16, AHALF), BF16),
            pltpu.VMEM((HALVES, 7, NP, 16, BHALF), BF16),
            pltpu.VMEM((8, 16, AHALF), F32),
            pltpu.VMEM((HALVES, NP, 16, BHALF), F32),
            pltpu.VMEM((8, 16, AHALF), BF16),
            pltpu.VMEM((8, 16, BHALF), BF16),
            pltpu.VMEM((7, 16, AHALF), BF16),
            pltpu.VMEM((7, 16, BHALF), BF16),
            dma((CHUNKS,)), dma((2,)), dma((2,)), dma((3,)), dma((3,)),
            dma((7,)), dma((7,)), dma((14,)), dma((14,)), dma((7,)), dma((7,)), dma((7,)), dma((7,)),
        ],
        compiler_params=pltpu.CompilerParams(
            collective_id=0, has_side_effects=True, vmem_limit_bytes=56 * 1024 * 1024
        ),
    )(jacobian, misfit.reshape(16, 128), taps.reshape(1, ORDER))
    fisher, newton = pl.pallas_call(
        outputs,
        out_shape=(jax.ShapeDtypeStruct((8, WIDTH), F32), jax.ShapeDtypeStruct((1, 8), F32)),
        in_specs=[vmem],
        out_specs=(vmem, vmem),
    )(rows)
    return fisher, newton.reshape(8)


def solution(mesh):
    in_specs = (P(("net", "tm"), None), P(("net", "tm")), P("net"))
    out_specs = (P(("net", "tm"), None), P(("net", "tm")))
    return jax.shard_map(shards, mesh=mesh, in_specs=in_specs, out_specs=out_specs, check_vma=False)
```

```python
import jax
import jax.numpy as jnp
from jax import lax
from jax.experimental import pallas as pl
from jax.experimental.pallas import tpu as pltpu
from jax.sharding import PartitionSpec as P

NX, NZ, NY, NC = 4, 8, 2, 2
NU = NX * NY
OWNERS = NX * NZ * NY * NC
MESH = pl.DeviceIdType.MESH
BF16, F32 = jnp.bfloat16, jnp.float32

ROWS, WIDTH, ORDER = 2048, 1024, 64
BLOCK = 192
GREET = 8
BOUNDS = [0, 512, 1024, 1536, 2048]
CHUNKS = len(BOUNDS) - 1
KROWS = 256
MROWS = 256
ACOLS = 256
BCOLS = WIDTH - ACOLS
AHALF, BHALF = ACOLS // 2, BCOLS // 2
TOTAL = ROWS * OWNERS
XY_STEPS = [(2, 0), (2, 1), (1, 0), (3, 0), (1, 1), (3, 1), (0, 1)]
Z_STEPS = [4, 3, 5, 2, 6, 1, 7]
HALVES, NP = 2, NZ // 2


def position(x, z, y, c):
    return ((lax.rem(x, NX) * NZ + lax.rem(z, NZ)) * NY + lax.rem(y, NY)) * NC + lax.rem(c, NC)


def folded(rows):
    half = rows.shape[1] // 2
    return jnp.concatenate([rows[:, :half], rows[:, half:]], axis=0)


def unfolded(piece):
    return jnp.concatenate([piece[:8], piece[8:]], axis=1)


def place_of(step):
    return (step - 2) % NZ


def beside(shape, base):
    r = lax.broadcasted_iota(jnp.int32, shape, 0)
    lane = lax.broadcasted_iota(jnp.int32, shape, 1) - base
    return lane == lax.rem(r + 1, 8), lane == lax.rem(r + 2, 8)


def two_terms(value):
    high = value.astype(BF16).astype(F32)
    return high, value - high


def place(rows, base, grad):
    one, two = beside(rows.shape, base)
    high, low = two_terms(grad)
    return jnp.where(one, high, jnp.where(two, low, rows))


def split_again(rows, base):
    one, two = beside(rows.shape, base)
    high, low = two_terms(jnp.sum(jnp.where(one | two, rows, 0.0), axis=0, keepdims=True))
    return jnp.where(one, high, jnp.where(two, low, rows))


def in_tiles(rows, first, change):
    if first < 0 or first * 128 >= rows.shape[1]:
        return rows
    low, high = first * 128, first * 128 + 256
    parts = [rows[:, :low], change(rows[:, low:high]), rows[:, high:]]
    return jnp.concatenate([part for part in parts if part.shape[1]], axis=1)


def kernel(
    jac, mis, taps, rows_out,
    xbuf, white, white_t, wm_rows, mis_tail, acc,
    keep_a, keep_b, core_sa, core_sb, core_ra, core_rb,
    s1a, s1b, r1a, r1b, a2, b2, s2a, s2b, r2a, r2b,
    load_sem, halo_ss, halo_rs, core_ss, core_rs,
    s1a_ss, s1a_rs, s1b_ss, s1b_rs, s2a_ss, s2a_rs, s2b_ss, s2b_rs,
):
    me = lax.axis_index("tm")
    x, z, y, c = me // (NZ * NY * NC), (me // (NY * NC)) % NZ, (me // NC) % NY, me % NC
    sibling = position(x, z, y, c + 1)
    after, before = lax.rem(me + 1, OWNERS), lax.rem(me + OWNERS - 1, OWNERS)
    xy_dev = [position(x + dx, z, y + dy, c) for dx, dy in XY_STEPS]
    xy_own = [lax.rem(x + dx, NX) * NY + lax.rem(y + dy, NY) for dx, dy in XY_STEPS]
    z_dev = [position(x, z + dz, y, c) for dz in Z_STEPS]
    z_own = [lax.rem(z + dz, NZ) for dz in Z_STEPS]
    u = x * NY + y
    z_place = [lax.rem(zo + 2 * NZ - z - 2, NZ) for zo in range(NZ)]
    z_rows = [p // NP * 512 + p % NP * 32 for p in z_place]
    z_at = [lax.rem(z + 2 + p, NZ) for p in range(NZ)]

    loads = []
    for i, (low, high) in enumerate(zip(BOUNDS[:-1], BOUNDS[1:])):
        loads.append(pltpu.make_async_copy(
            jac.at[pl.ds(low, high - low)], xbuf.at[pl.ds(ORDER + low, high - low)], load_sem.at[i]
        ))
    for load in loads[::-1]:
        load.start()

    barrier = pltpu.get_barrier_semaphore()
    partners = [sibling, after, before] + xy_dev + z_dev
    for device in partners:
        pl.semaphore_signal(barrier, inc=1, device_id={"tm": device}, device_id_type=MESH)

    coef = jnp.broadcast_to(taps[...].astype(BF16), (16, ORDER))
    lag_of = lax.broadcasted_iota(jnp.int32, (ORDER, 256), 0)
    lane_of = lax.broadcasted_iota(jnp.int32, (ORDER, 256), 1)
    flip = (lag_of + lane_of == ORDER - 1).astype(F32).astype(BF16)
    first = jnp.dot(coef, flip, preferred_element_type=F32)[:1]
    lane = lax.broadcasted_iota(jnp.int32, (1, 256), 1)
    first = jnp.where(lane == ORDER, 1.0, -first)
    matrix = pltpu.roll(jnp.broadcast_to(first, (BLOCK, 256)), 0, 1, stride=1, stride_axis=0).astype(BF16)
    mis_matrix = pltpu.roll(jnp.broadcast_to(first, (128, 256)), ORDER, 1, stride=1, stride_axis=0).astype(BF16)

    def whiten_misfit(tail):
        here = mis[...].astype(F32)
        row_of = lax.broadcasted_iota(jnp.int32, (16, 128), 0)
        previous = jnp.where(row_of == 0, pltpu.roll(tail, 1, 0), pltpu.roll(here, 1, 0))
        both = jnp.concatenate([previous, here], axis=1).astype(BF16)
        return lax.dot_general(both, mis_matrix, (((1,), (1,)), ((), ())), preferred_element_type=F32)

    def put_misfit(white_mis, i):
        wm_rows[:, i * 128 : (i + 1) * 128] = jnp.broadcast_to(white_mis[i : i + 1], (16, 128)).astype(BF16)

    white_mis = whiten_misfit(jnp.zeros((16, 128), F32))
    for i in range(1, 16):
        put_misfit(white_mis, i)

    def whiten(start, rows):
        out = jnp.dot(
            matrix[:rows, : rows + ORDER], xbuf[start : start + rows + ORDER], preferred_element_type=F32
        )
        white[start : start + rows] = out.astype(BF16)

    def transpose(i):
        block = white[i * KROWS : (i + 1) * KROWS].T
        for zo in range(NZ):
            for xo in range(NX):
                rows = pl.ds(pl.multiple_of(z_rows[zo] + xo * 128, 32), 32)
                white_t[rows, i * KROWS : (i + 1) * KROWS] = block[xo * 256 + zo * 32 : xo * 256 + zo * 32 + 32]

    halo = pltpu.make_async_remote_copy(
        src_ref=jac.at[pl.ds(ROWS - ORDER, ORDER)], dst_ref=xbuf.at[pl.ds(0, ORDER)],
        send_sem=halo_ss.at[0], recv_sem=halo_rs.at[0], device_id={"tm": after}, device_id_type=MESH,
    )
    mis_halo = pltpu.make_async_remote_copy(
        src_ref=mis, dst_ref=mis_tail,
        send_sem=halo_ss.at[1], recv_sem=halo_rs.at[1], device_id={"tm": after}, device_id_type=MESH,
    )

    ready, turned = CHUNKS, ROWS // KROWS
    for start in list(range(0, ROWS, BLOCK))[:0:-1]:
        rows = min(BLOCK, ROWS - start)
        while BOUNDS[ready] > start - ORDER:
            ready -= 1
            loads[ready].wait()
        if start == GREET * BLOCK:
            pl.semaphore_wait(barrier, len(partners))

            @pl.when(me < OWNERS - 1)
            def _():
                halo.start()
                mis_halo.start()

        whiten(start, rows)
        while (turned - 1) * KROWS >= start:
            turned -= 1
            transpose(turned)
    while ready > 0:
        ready -= 1
        loads[ready].wait()

    def product(row, rows, left, right, low, high):
        parts = []
        for i in range(row, row + rows, MROWS):
            lhs = white_t[i : i + MROWS, low:high]
            if i + MROWS == row + rows:
                lhs = jnp.concatenate([lhs, wm_rows[:, low:high]], axis=0)
            parts.append(jnp.dot(lhs, white[low:high, left:right], preferred_element_type=F32))
        return jnp.concatenate(parts, axis=0)

    def gram_a(low, high):
        return product(0, WIDTH, 0, ACOLS, low, high)

    def gram_b(half, low, high):
        return product(half * 512, 512, ACOLS, WIDTH, low, high)

    acc[...] = gram_b(0, KROWS, ROWS)

    @pl.when(me > 0)
    def _():
        halo.wait_recv()
        mis_halo.wait_recv()

    @pl.when(me == 0)
    def _():
        xbuf[:ORDER] = jnp.zeros((ORDER, WIDTH), BF16)
        mis_tail[...] = jnp.zeros_like(mis_tail)

    whiten(0, BLOCK)
    transpose(0)
    put_misfit(whiten_misfit(mis_tail[...].astype(F32)), 0)

    def to_sibling(src, dst, k):
        return pltpu.make_async_remote_copy(
            src_ref=src, dst_ref=dst, send_sem=core_ss.at[k], recv_sem=core_rs.at[k],
            device_id={"tm": sibling}, device_id_type=MESH,
        )

    mine_first = c == 0

    def base_of(p, yo, side):
        return z_at[p] * 32 + (yo * NC + side) * 8

    def deal(rows, grad, first, p, yo, keep, send, index):
        pair = []
        for side in range(NC):
            part = rows[side * 8 : side * 8 + 8]

            def change(tiles, side=side):
                return place(tiles, base_of(p, yo, side), grad[:, first * 128 : first * 128 + 256])

            pair.append(folded(in_tiles(part, first, change)))
        keep[index] = jnp.where(mine_first, pair[0], pair[1])
        send[index] = jnp.where(mine_first, pair[1], pair[0]).astype(BF16)

    def both_cores(keep, received, index, first, p, yo):
        rows = keep[index] + received[index].astype(F32)
        if first < 0 or first * 128 >= 2 * rows.shape[1]:
            return rows.astype(BF16)
        rows = in_tiles(unfolded(rows), first, lambda tiles: split_again(tiles, base_of(p, yo, c)))
        return folded(rows).astype(BF16)

    stage1a, stage1b, core_b = [], [], []

    def finish_b(half, out):
        for xo in range(NX):
            for pp in range(NP):
                for yo in range(NY):
                    row = xo * 128 + pp * 32 + yo * 16
                    deal(
                        out[row : row + 16], out[512:513], xo * 2 - 2, half * NP + pp, yo,
                        keep_b, core_sb, (half * NU + xo * NY + yo) * NP + pp,
                    )
        span = pl.ds(half * NU * NP, NU * NP)
        copy = to_sibling(core_sb.at[span], core_rb.at[span], 1 + half)
        copy.start()
        core_b.append(copy)

    def send_b(half):
        core_b[half].wait_recv()
        for xo in range(NX):
            for yo in range(NY):
                for pp in range(NP):
                    index = (half * NU + xo * NY + yo) * NP + pp
                    s1b[index] = both_cores(keep_b, core_rb, index, xo * 2 - 2, half * NP + pp, yo)
        for k, (device, own) in enumerate(zip(xy_dev, xy_own)):
            copy = pltpu.make_async_remote_copy(
                src_ref=s1b.at[pl.ds((half * NU + own) * NP, NP)], dst_ref=r1b.at[half, k],
                send_sem=s1b_ss.at[half * 7 + k], recv_sem=s1b_rs.at[half * 7 + k],
                device_id={"tm": device}, device_id_type=MESH,
            )
            copy.start()
            stage1b.append(copy)

    finish_b(0, acc[...] + gram_b(0, 0, KROWS))

    out = gram_a(0, ROWS)
    for half in range(HALVES):
        for xo in range(NX):
            for pp in range(NP):
                for yo in range(NY):
                    row = half * 512 + xo * 128 + pp * 32 + yo * 16
                    p = half * NP + pp
                    deal(
                        out[row : row + 16], out[WIDTH : WIDTH + 1], xo * 2, p, yo,
                        keep_a, core_sa, p * NU + xo * NY + yo,
                    )
    core_a = to_sibling(core_sa, core_ra, 0)
    core_a.start()
    send_b(0)

    finish_b(1, gram_b(1, 0, ROWS))

    core_a.wait_recv()
    for p in range(NZ):
        for xo in range(NX):
            for yo in range(NY):
                index = p * NU + xo * NY + yo
                s1a[index] = both_cores(keep_a, core_ra, index, xo * 2, p, yo)
    for k, (device, step) in enumerate(zip(z_dev, Z_STEPS)):
        copy = pltpu.make_async_remote_copy(
            src_ref=s1a.at[pl.ds(place_of(step) * NU, NU)], dst_ref=r1a.at[k],
            send_sem=s1a_ss.at[k], recv_sem=s1a_rs.at[k], device_id={"tm": device}, device_id_type=MESH,
        )
        copy.start()
        stage1a.append(copy)
    send_b(1)

    stage2b = {}

    def pass_b(half):
        span = pl.ds((half * NU + u) * NP, NP)
        b2[half] = keep_b[span] + core_rb[span].astype(F32)
        for k in range(7):
            stage1b[half * 7 + k].wait_recv()
            b2[half] += r1b[half, k].astype(F32)
        for pp in range(NP):
            p = half * NP + pp
            lane = x * 256 - ACOLS + base_of(p, y, c)
            s2b[p] = folded(split_again(unfolded(b2[half, pp]), lane)).astype(BF16)
        for k, (device, step) in enumerate(zip(z_dev, Z_STEPS)):
            p = place_of(step)
            if p // NP == half:
                copy = pltpu.make_async_remote_copy(
                    src_ref=s2b.at[p], dst_ref=r2b.at[k],
                    send_sem=s2b_ss.at[k], recv_sem=s2b_rs.at[k], device_id={"tm": device}, device_id_type=MESH,
                )
                copy.start()
                stage2b[k] = copy

    pass_b(0)

    span = pl.ds(place_of(0) * NU, NU)
    a2[...] = keep_a[span] + core_ra[span].astype(F32)
    for k, copy in enumerate(stage1a):
        copy.wait_recv()
        a2[...] += r1a[k].astype(F32)
    for xo in range(NX):
        for yo in range(NY):
            rows = a2[xo * NY + yo]
            if xo == 0:
                rows = folded(split_again(unfolded(rows), base_of(place_of(0), yo, c)))
            s2a[xo * NY + yo] = rows.astype(BF16)
    stage2a = []
    for k, (device, own) in enumerate(zip(xy_dev, xy_own)):
        copy = pltpu.make_async_remote_copy(
            src_ref=s2a.at[own], dst_ref=r2a.at[k],
            send_sem=s2a_ss.at[k], recv_sem=s2a_rs.at[k], device_id={"tm": device}, device_id_type=MESH,
        )
        copy.start()
        stage2a.append(copy)

    pass_b(1)

    last_a, last_b = a2[u], b2[place_of(0) // NP, place_of(0) % NP]
    for k, copy in enumerate(stage2a):
        copy.wait_recv()
        last_a = last_a + r2a[k].astype(F32)

    @pl.when(me < OWNERS - 1)
    def _():
        halo.wait_send()
        mis_halo.wait_send()

    for copy in [core_a] + core_b + stage1a + stage1b + stage2a:
        copy.wait_send()

    for k, copy in stage2b.items():
        copy.wait_recv()
        last_b = last_b + r2b[k].astype(F32)
    rows_out[:, :ACOLS] = unfolded(last_a)
    rows_out[:, ACOLS:] = unfolded(last_b)

    for copy in stage2b.values():
        copy.wait_send()


def outputs(rows_ref, fisher, newton):
    rows = rows_ref[...]
    r = lax.broadcasted_iota(jnp.int32, rows.shape, 0)
    col = lax.broadcasted_iota(jnp.int32, rows.shape, 1) - lax.axis_index("tm") * 8
    one, two, on = col == lax.rem(r + 1, 8), col == lax.rem(r + 2, 8), col == r

    def picked(mask, values):
        return jnp.broadcast_to(jnp.sum(jnp.where(mask, values, 0.0), axis=1, keepdims=True), (8, 128))

    grad = pltpu.roll(picked(one, rows), 1, 0) + pltpu.roll(picked(two, rows), 2, 0)
    diagonal = picked(on, rows)
    mirror_one = picked(on, pltpu.roll(rows, 7, 0))[:, :1]
    mirror_two = picked(on, pltpu.roll(rows, 6, 0))[:, :1]
    fisher[...] = jnp.where(one, mirror_one, jnp.where(two, mirror_two, rows)) * (1.0 / TOTAL)
    r8 = lax.broadcasted_iota(jnp.int32, (8, 128), 0)
    c8 = lax.broadcasted_iota(jnp.int32, (8, 128), 1)
    newton[...] = jnp.sum(jnp.where(r8 == c8, grad / diagonal, 0.0), axis=0, keepdims=True)[:, :8]


def shards(jacobian, misfit, taps):
    dma = pltpu.SemaphoreType.DMA
    vmem = pl.BlockSpec(memory_space=pltpu.VMEM)
    rows = pl.pallas_call(
        kernel,
        out_shape=jax.ShapeDtypeStruct((8, WIDTH), F32),
        in_specs=[pl.BlockSpec(memory_space=pl.ANY), vmem, vmem],
        out_specs=vmem,
        scratch_shapes=[
            pltpu.VMEM((ROWS + ORDER, WIDTH), BF16),
            pltpu.VMEM((ROWS, WIDTH), BF16),
            pltpu.VMEM((WIDTH, ROWS), BF16),
            pltpu.VMEM((16, ROWS), BF16),
            pltpu.VMEM((16, 128), BF16),
            pltpu.VMEM((512 + 16, BCOLS), F32),
            pltpu.VMEM((64, 16, AHALF), F32),
            pltpu.VMEM((64, 16, BHALF), F32),
            pltpu.VMEM((64, 16, AHALF), BF16),
            pltpu.VMEM((64, 16, BHALF), BF16),
            pltpu.VMEM((64, 16, AHALF), BF16),
            pltpu.VMEM((64, 16, BHALF), BF16),
            pltpu.VMEM((64, 16, AHALF), BF16),
            pltpu.VMEM((64, 16, BHALF), BF16),
            pltpu.VMEM((7, 8, 16, AHALF), BF16),
            pltpu.VMEM((HALVES, 7, NP, 16, BHALF), BF16),
            pltpu.VMEM((8, 16, AHALF), F32),
            pltpu.VMEM((HALVES, NP, 16, BHALF), F32),
            pltpu.VMEM((8, 16, AHALF), BF16),
            pltpu.VMEM((8, 16, BHALF), BF16),
            pltpu.VMEM((7, 16, AHALF), BF16),
            pltpu.VMEM((7, 16, BHALF), BF16),
            dma((CHUNKS,)), dma((2,)), dma((2,)), dma((3,)), dma((3,)),
            dma((7,)), dma((7,)), dma((14,)), dma((14,)), dma((7,)), dma((7,)), dma((7,)), dma((7,)),
        ],
        compiler_params=pltpu.CompilerParams(
            collective_id=0, has_side_effects=True, vmem_limit_bytes=56 * 1024 * 1024
        ),
    )(jacobian, misfit.reshape(16, 128), taps.reshape(1, ORDER))
    fisher, newton = pl.pallas_call(
        outputs,
        out_shape=(jax.ShapeDtypeStruct((8, WIDTH), F32), jax.ShapeDtypeStruct((1, 8), F32)),
        in_specs=[vmem],
        out_specs=(vmem, vmem),
    )(rows)
    return fisher, newton.reshape(8)


def solution(mesh):
    in_specs = (P(("net", "tm"), None), P(("net", "tm")), P("net"))
    out_specs = (P(("net", "tm"), None), P(("net", "tm")))
    return jax.shard_map(shards, mesh=mesh, in_specs=in_specs, out_specs=out_specs, check_vma=False)
```

```python
import jax
import jax.numpy as jnp
from jax import lax
from jax.experimental import pallas as pl
from jax.experimental.pallas import tpu as pltpu
from jax.sharding import PartitionSpec as P

NX, NZ, NY, NC = 4, 8, 2, 2
NU = NX * NY
OWNERS = NX * NZ * NY * NC
MESH = pl.DeviceIdType.MESH
BF16, F32 = jnp.bfloat16, jnp.float32

ROWS, WIDTH, ORDER = 2048, 1024, 64
BLOCK = 192
GREET = 8
BOUNDS = [0, 512, 1024, 1536, 2048]
CHUNKS = len(BOUNDS) - 1
KROWS = 256
MROWS = 256
ACOLS = 256
BCOLS = WIDTH - ACOLS
AHALF, BHALF = ACOLS // 2, BCOLS // 2
TOTAL = ROWS * OWNERS
XY_STEPS = [(2, 0), (2, 1), (1, 0), (3, 0), (1, 1), (3, 1), (0, 1)]
Z_STEPS = [4, 3, 5, 2, 6, 1, 7]
HALVES, NP = 2, NZ // 2


def position(x, z, y, c):
    return ((lax.rem(x, NX) * NZ + lax.rem(z, NZ)) * NY + lax.rem(y, NY)) * NC + lax.rem(c, NC)


def folded(rows):
    half = rows.shape[1] // 2
    return jnp.concatenate([rows[:, :half], rows[:, half:]], axis=0)


def unfolded(piece):
    return jnp.concatenate([piece[:8], piece[8:]], axis=1)


def place_of(step):
    return (step - 2) % NZ


def beside(shape, base):
    r = lax.broadcasted_iota(jnp.int32, shape, 0)
    lane = lax.broadcasted_iota(jnp.int32, shape, 1) - base
    return lane == lax.rem(r + 1, 8), lane == lax.rem(r + 2, 8)


def two_terms(value):
    high = value.astype(BF16).astype(F32)
    return high, value - high


def place(rows, base, grad):
    one, two = beside(rows.shape, base)
    high, low = two_terms(grad)
    return jnp.where(one, high, jnp.where(two, low, rows))


def split_again(rows, base):
    one, two = beside(rows.shape, base)
    high, low = two_terms(jnp.sum(jnp.where(one | two, rows, 0.0), axis=0, keepdims=True))
    return jnp.where(one, high, jnp.where(two, low, rows))


def in_tiles(rows, first, change):
    if first < 0 or first * 128 >= rows.shape[1]:
        return rows
    low, high = first * 128, first * 128 + 256
    parts = [rows[:, :low], change(rows[:, low:high]), rows[:, high:]]
    return jnp.concatenate([part for part in parts if part.shape[1]], axis=1)


def kernel(
    jac, mis_in, taps_in, rows_out,
    mis, taps, xbuf, white, white_t, wm_rows, mis_tail, acc,
    keep_a, keep_b, core_sa, core_sb, core_ra, core_rb,
    s1a, s1b, r1a, r1b, a2, b2, s2a, s2b, r2a, r2b,
    load_sem, halo_ss, halo_rs, core_ss, core_rs,
    s1a_ss, s1a_rs, s1b_ss, s1b_rs, s2a_ss, s2a_rs, s2b_ss, s2b_rs,
):
    me = lax.axis_index("tm")
    x, z, y, c = me // (NZ * NY * NC), (me // (NY * NC)) % NZ, (me // NC) % NY, me % NC
    sibling = position(x, z, y, c + 1)
    after, before = lax.rem(me + 1, OWNERS), lax.rem(me + OWNERS - 1, OWNERS)
    xy_dev = [position(x + dx, z, y + dy, c) for dx, dy in XY_STEPS]
    xy_own = [lax.rem(x + dx, NX) * NY + lax.rem(y + dy, NY) for dx, dy in XY_STEPS]
    z_dev = [position(x, z + dz, y, c) for dz in Z_STEPS]
    z_own = [lax.rem(z + dz, NZ) for dz in Z_STEPS]
    u = x * NY + y
    z_place = [lax.rem(zo + 2 * NZ - z - 2, NZ) for zo in range(NZ)]
    z_rows = [p // NP * 512 + p % NP * 32 for p in z_place]
    z_at = [lax.rem(z + 2 + p, NZ) for p in range(NZ)]

    loads = []
    for i, (low, high) in enumerate(zip(BOUNDS[:-1], BOUNDS[1:])):
        loads.append(pltpu.make_async_copy(
            jac.at[pl.ds(low, high - low)], xbuf.at[pl.ds(ORDER + low, high - low)], load_sem.at[i]
        ))

    small = [
        pltpu.make_async_copy(taps_in, taps, load_sem.at[CHUNKS]),
        pltpu.make_async_copy(mis_in, mis, load_sem.at[CHUNKS + 1]),
    ]
    for load in small + loads[::-1]:
        load.start()

    barrier = pltpu.get_barrier_semaphore()
    partners = [sibling, after, before] + xy_dev + z_dev
    for device in partners:
        pl.semaphore_signal(barrier, inc=1, device_id={"tm": device}, device_id_type=MESH)

    for load in small:
        load.wait()

    coef = jnp.broadcast_to(taps[...].astype(BF16), (16, ORDER))
    lag_of = lax.broadcasted_iota(jnp.int32, (ORDER, 256), 0)
    lane_of = lax.broadcasted_iota(jnp.int32, (ORDER, 256), 1)
    flip = (lag_of + lane_of == ORDER - 1).astype(F32).astype(BF16)
    first = jnp.dot(coef, flip, preferred_element_type=F32)[:1]
    lane = lax.broadcasted_iota(jnp.int32, (1, 256), 1)
    first = jnp.where(lane == ORDER, 1.0, -first)
    matrix = pltpu.roll(jnp.broadcast_to(first, (BLOCK, 256)), 0, 1, stride=1, stride_axis=0).astype(BF16)
    mis_matrix = pltpu.roll(jnp.broadcast_to(first, (128, 256)), ORDER, 1, stride=1, stride_axis=0).astype(BF16)

    def whiten_misfit(tail):
        here = mis[...].astype(F32)
        row_of = lax.broadcasted_iota(jnp.int32, (16, 128), 0)
        previous = jnp.where(row_of == 0, pltpu.roll(tail, 1, 0), pltpu.roll(here, 1, 0))
        both = jnp.concatenate([previous, here], axis=1).astype(BF16)
        return lax.dot_general(both, mis_matrix, (((1,), (1,)), ((), ())), preferred_element_type=F32)

    def put_misfit(white_mis, i):
        wm_rows[:, i * 128 : (i + 1) * 128] = jnp.broadcast_to(white_mis[i : i + 1], (16, 128)).astype(BF16)

    white_mis = whiten_misfit(jnp.zeros((16, 128), F32))
    for i in range(1, 16):
        put_misfit(white_mis, i)

    def whiten(start, rows):
        out = jnp.dot(
            matrix[:rows, : rows + ORDER], xbuf[start : start + rows + ORDER], preferred_element_type=F32
        )
        white[start : start + rows] = out.astype(BF16)

    def transpose(i):
        block = white[i * KROWS : (i + 1) * KROWS].T
        for zo in range(NZ):
            for xo in range(NX):
                pass
        white_t[:, i * KROWS : (i + 1) * KROWS] = block

    halo = pltpu.make_async_remote_copy(
        src_ref=jac.at[pl.ds(ROWS - ORDER, ORDER)], dst_ref=xbuf.at[pl.ds(0, ORDER)],
        send_sem=halo_ss.at[0], recv_sem=halo_rs.at[0], device_id={"tm": after}, device_id_type=MESH,
    )
    mis_halo = pltpu.make_async_remote_copy(
        src_ref=mis_in, dst_ref=mis_tail,
        send_sem=halo_ss.at[1], recv_sem=halo_rs.at[1], device_id={"tm": after}, device_id_type=MESH,
    )

    ready, turned = CHUNKS, ROWS // KROWS
    for start in list(range(0, ROWS, BLOCK))[:0:-1]:
        rows = min(BLOCK, ROWS - start)
        while BOUNDS[ready] > start - ORDER:
            ready -= 1
            loads[ready].wait()
        if start == GREET * BLOCK:
            pl.semaphore_wait(barrier, len(partners))

            @pl.when(me < OWNERS - 1)
            def _():
                halo.start()
                mis_halo.start()

        whiten(start, rows)
        while (turned - 1) * KROWS >= start:
            turned -= 1
            transpose(turned)
    while ready > 0:
        ready -= 1
        loads[ready].wait()

    def z_group(row):
        half, xo, pp = row // 512, row // 128 % NX, row // 32 % NP
        return pl.ds(pl.multiple_of(xo * 256 + z_at[half * NP + pp] * 32, 32), 32)

    def product(row, rows, left, right, low, high):
        parts = []
        for i in range(row, row + rows, MROWS):
            lhs = jnp.concatenate(
                [white_t[z_group(j), low:high] for j in range(i, i + MROWS, 32)], axis=0
            )
            if i + MROWS == row + rows:
                lhs = jnp.concatenate([lhs, wm_rows[:, low:high]], axis=0)
            parts.append(jnp.dot(lhs, white[low:high, left:right], preferred_element_type=F32))
        return jnp.concatenate(parts, axis=0)

    def gram_a(low, high):
        return product(0, WIDTH, 0, ACOLS, low, high)

    def gram_b(half, low, high):
        return product(half * 512, 512, ACOLS, WIDTH, low, high)

    acc[...] = gram_b(0, KROWS, ROWS)

    @pl.when(me > 0)
    def _():
        halo.wait_recv()
        mis_halo.wait_recv()

    @pl.when(me == 0)
    def _():
        xbuf[:ORDER] = jnp.zeros((ORDER, WIDTH), BF16)
        mis_tail[...] = jnp.zeros_like(mis_tail)

    whiten(0, BLOCK)
    transpose(0)
    put_misfit(whiten_misfit(mis_tail[...].astype(F32)), 0)

    def to_sibling(src, dst, k):
        return pltpu.make_async_remote_copy(
            src_ref=src, dst_ref=dst, send_sem=core_ss.at[k], recv_sem=core_rs.at[k],
            device_id={"tm": sibling}, device_id_type=MESH,
        )

    mine_first = c == 0

    def base_of(p, yo, side):
        return z_at[p] * 32 + (yo * NC + side) * 8

    def deal(rows, grad, first, p, yo, keep, send, index):
        pair = []
        for side in range(NC):
            part = rows[side * 8 : side * 8 + 8]

            def change(tiles, side=side):
                return place(tiles, base_of(p, yo, side), grad[:, first * 128 : first * 128 + 256])

            pair.append(folded(in_tiles(part, first, change)))
        keep[index] = jnp.where(mine_first, pair[0], pair[1])
        send[index] = jnp.where(mine_first, pair[1], pair[0]).astype(BF16)

    def both_cores(keep, received, index, first, p, yo):
        rows = keep[index] + received[index].astype(F32)
        if first < 0 or first * 128 >= 2 * rows.shape[1]:
            return rows.astype(BF16)
        rows = in_tiles(unfolded(rows), first, lambda tiles: split_again(tiles, base_of(p, yo, c)))
        return folded(rows).astype(BF16)

    stage1a, stage1b, core_b = [], [], []

    def finish_b(half, out):
        for xo in range(NX):
            for pp in range(NP):
                for yo in range(NY):
                    row = xo * 128 + pp * 32 + yo * 16
                    deal(
                        out[row : row + 16], out[512:513], xo * 2 - 2, half * NP + pp, yo,
                        keep_b, core_sb, (half * NU + xo * NY + yo) * NP + pp,
                    )
        span = pl.ds(half * NU * NP, NU * NP)
        copy = to_sibling(core_sb.at[span], core_rb.at[span], 1 + half)
        copy.start()
        core_b.append(copy)

    def send_b(half):
        core_b[half].wait_recv()
        for xo in range(NX):
            for yo in range(NY):
                for pp in range(NP):
                    index = (half * NU + xo * NY + yo) * NP + pp
                    s1b[index] = both_cores(keep_b, core_rb, index, xo * 2 - 2, half * NP + pp, yo)
        for k, (device, own) in enumerate(zip(xy_dev, xy_own)):
            copy = pltpu.make_async_remote_copy(
                src_ref=s1b.at[pl.ds((half * NU + own) * NP, NP)], dst_ref=r1b.at[half, k],
                send_sem=s1b_ss.at[half * 7 + k], recv_sem=s1b_rs.at[half * 7 + k],
                device_id={"tm": device}, device_id_type=MESH,
            )
            copy.start()
            stage1b.append(copy)

    finish_b(0, acc[...] + gram_b(0, 0, KROWS))

    out = gram_a(0, ROWS)
    for half in range(HALVES):
        for xo in range(NX):
            for pp in range(NP):
                for yo in range(NY):
                    row = half * 512 + xo * 128 + pp * 32 + yo * 16
                    p = half * NP + pp
                    deal(
                        out[row : row + 16], out[WIDTH : WIDTH + 1], xo * 2, p, yo,
                        keep_a, core_sa, p * NU + xo * NY + yo,
                    )
    core_a = to_sibling(core_sa, core_ra, 0)
    core_a.start()
    send_b(0)

    finish_b(1, gram_b(1, 0, ROWS))

    core_a.wait_recv()
    for p in range(NZ):
        for xo in range(NX):
            for yo in range(NY):
                index = p * NU + xo * NY + yo
                s1a[index] = both_cores(keep_a, core_ra, index, xo * 2, p, yo)
    for k, (device, step) in enumerate(zip(z_dev, Z_STEPS)):
        copy = pltpu.make_async_remote_copy(
            src_ref=s1a.at[pl.ds(place_of(step) * NU, NU)], dst_ref=r1a.at[k],
            send_sem=s1a_ss.at[k], recv_sem=s1a_rs.at[k], device_id={"tm": device}, device_id_type=MESH,
        )
        copy.start()
        stage1a.append(copy)
    send_b(1)

    stage2b = {}

    def pass_b(half):
        span = pl.ds((half * NU + u) * NP, NP)
        b2[half] = keep_b[span] + core_rb[span].astype(F32)
        for k in range(7):
            stage1b[half * 7 + k].wait_recv()
            b2[half] += r1b[half, k].astype(F32)
        for pp in range(NP):
            p = half * NP + pp
            lane = x * 256 - ACOLS + base_of(p, y, c)
            s2b[p] = folded(split_again(unfolded(b2[half, pp]), lane)).astype(BF16)
        for k, (device, step) in enumerate(zip(z_dev, Z_STEPS)):
            p = place_of(step)
            if p // NP == half:
                copy = pltpu.make_async_remote_copy(
                    src_ref=s2b.at[p], dst_ref=r2b.at[k],
                    send_sem=s2b_ss.at[k], recv_sem=s2b_rs.at[k], device_id={"tm": device}, device_id_type=MESH,
                )
                copy.start()
                stage2b[k] = copy

    pass_b(0)

    span = pl.ds(place_of(0) * NU, NU)
    a2[...] = keep_a[span] + core_ra[span].astype(F32)
    for k, copy in enumerate(stage1a):
        copy.wait_recv()
        a2[...] += r1a[k].astype(F32)
    for xo in range(NX):
        for yo in range(NY):
            rows = a2[xo * NY + yo]
            if xo == 0:
                rows = folded(split_again(unfolded(rows), base_of(place_of(0), yo, c)))
            s2a[xo * NY + yo] = rows.astype(BF16)
    stage2a = []
    for k, (device, own) in enumerate(zip(xy_dev, xy_own)):
        copy = pltpu.make_async_remote_copy(
            src_ref=s2a.at[own], dst_ref=r2a.at[k],
            send_sem=s2a_ss.at[k], recv_sem=s2a_rs.at[k], device_id={"tm": device}, device_id_type=MESH,
        )
        copy.start()
        stage2a.append(copy)

    pass_b(1)

    last_a, last_b = a2[u], b2[place_of(0) // NP, place_of(0) % NP]
    for k, copy in enumerate(stage2a):
        copy.wait_recv()
        last_a = last_a + r2a[k].astype(F32)

    @pl.when(me < OWNERS - 1)
    def _():
        halo.wait_send()
        mis_halo.wait_send()

    for copy in [core_a] + core_b + stage1a + stage1b + stage2a:
        copy.wait_send()

    for k, copy in stage2b.items():
        copy.wait_recv()
        last_b = last_b + r2b[k].astype(F32)
    rows_out[:, :ACOLS] = unfolded(last_a)
    rows_out[:, ACOLS:] = unfolded(last_b)

    for copy in stage2b.values():
        copy.wait_send()


def outputs(rows_ref, fisher, newton):
    rows = rows_ref[...]
    r = lax.broadcasted_iota(jnp.int32, rows.shape, 0)
    col = lax.broadcasted_iota(jnp.int32, rows.shape, 1) - lax.axis_index("tm") * 8
    one, two, on = col == lax.rem(r + 1, 8), col == lax.rem(r + 2, 8), col == r

    def picked(mask, values):
        return jnp.broadcast_to(jnp.sum(jnp.where(mask, values, 0.0), axis=1, keepdims=True), (8, 128))

    grad = pltpu.roll(picked(one, rows), 1, 0) + pltpu.roll(picked(two, rows), 2, 0)
    diagonal = picked(on, rows)
    mirror_one = picked(on, pltpu.roll(rows, 7, 0))[:, :1]
    mirror_two = picked(on, pltpu.roll(rows, 6, 0))[:, :1]
    fisher[...] = jnp.where(one, mirror_one, jnp.where(two, mirror_two, rows)) * (1.0 / TOTAL)
    r8 = lax.broadcasted_iota(jnp.int32, (8, 128), 0)
    c8 = lax.broadcasted_iota(jnp.int32, (8, 128), 1)
    newton[...] = jnp.sum(jnp.where(r8 == c8, grad / diagonal, 0.0), axis=0, keepdims=True)[:, :8]


def shards(jacobian, misfit, taps):
    dma = pltpu.SemaphoreType.DMA
    vmem = pl.BlockSpec(memory_space=pltpu.VMEM)
    rows = pl.pallas_call(
        kernel,
        out_shape=pltpu.VMEM((8, WIDTH), F32),
        in_specs=[pl.BlockSpec(memory_space=pl.ANY)] * 3,
        out_specs=vmem,
        scratch_shapes=[
            pltpu.VMEM((16, 128), BF16),
            pltpu.VMEM((1, ORDER), F32),
            pltpu.VMEM((ROWS + ORDER, WIDTH), BF16),
            pltpu.VMEM((ROWS, WIDTH), BF16),
            pltpu.VMEM((WIDTH, ROWS), BF16),
            pltpu.VMEM((16, ROWS), BF16),
            pltpu.VMEM((16, 128), BF16),
            pltpu.VMEM((512 + 16, BCOLS), F32),
            pltpu.VMEM((64, 16, AHALF), F32),
            pltpu.VMEM((64, 16, BHALF), F32),
            pltpu.VMEM((64, 16, AHALF), BF16),
            pltpu.VMEM((64, 16, BHALF), BF16),
            pltpu.VMEM((64, 16, AHALF), BF16),
            pltpu.VMEM((64, 16, BHALF), BF16),
            pltpu.VMEM((64, 16, AHALF), BF16),
            pltpu.VMEM((64, 16, BHALF), BF16),
            pltpu.VMEM((7, 8, 16, AHALF), BF16),
            pltpu.VMEM((HALVES, 7, NP, 16, BHALF), BF16),
            pltpu.VMEM((8, 16, AHALF), F32),
            pltpu.VMEM((HALVES, NP, 16, BHALF), F32),
            pltpu.VMEM((8, 16, AHALF), BF16),
            pltpu.VMEM((8, 16, BHALF), BF16),
            pltpu.VMEM((7, 16, AHALF), BF16),
            pltpu.VMEM((7, 16, BHALF), BF16),
            dma((CHUNKS + 2,)), dma((2,)), dma((2,)), dma((3,)), dma((3,)),
            dma((7,)), dma((7,)), dma((14,)), dma((14,)), dma((7,)), dma((7,)), dma((7,)), dma((7,)),
        ],
        compiler_params=pltpu.CompilerParams(
            collective_id=0, has_side_effects=True, vmem_limit_bytes=56 * 1024 * 1024
        ),
    )(jacobian, misfit.reshape(16, 128), taps.reshape(1, ORDER))
    fisher, newton = pl.pallas_call(
        outputs,
        out_shape=(jax.ShapeDtypeStruct((8, WIDTH), F32), jax.ShapeDtypeStruct((1, 8), F32)),
        in_specs=[vmem],
        out_specs=(vmem, vmem),
    )(pltpu.with_memory_space_constraint(rows, pltpu.VMEM))
    return fisher, newton.reshape(8)


def solution(mesh):
    in_specs = (P(("net", "tm"), None), P(("net", "tm")), P("net"))
    out_specs = (P(("net", "tm"), None), P(("net", "tm")))
    return jax.shard_map(shards, mesh=mesh, in_specs=in_specs, out_specs=out_specs, check_vma=False)
```

```python
import jax
import jax.numpy as jnp
from jax import lax
from jax.experimental import pallas as pl
from jax.experimental.pallas import tpu as pltpu
from jax.sharding import PartitionSpec as P

NX, NZ, NY, NC = 4, 8, 2, 2
NU = NX * NY
OWNERS = NX * NZ * NY * NC
MESH = pl.DeviceIdType.MESH
BF16, F32 = jnp.bfloat16, jnp.float32

ROWS, WIDTH, ORDER = 2048, 1024, 64
BLOCK = 192
GREET = 8
BOUNDS = [0, 512, 1024, 1536, 2048]
CHUNKS = len(BOUNDS) - 1
KROWS = 256
MROWS = 256
ACOLS = 256
BCOLS = WIDTH - ACOLS
AHALF, BHALF = ACOLS // 2, BCOLS // 2
TOTAL = ROWS * OWNERS
XY_STEPS = [(0, 1), (2, 1), (1, 1), (3, 1), (2, 0), (1, 0), (3, 0)]
Z_STEPS = [4, 3, 5, 2, 6, 1, 7]
HALVES, NP = 2, NZ // 2


def position(x, z, y, c):
    return ((lax.rem(x, NX) * NZ + lax.rem(z, NZ)) * NY + lax.rem(y, NY)) * NC + lax.rem(c, NC)


def folded(rows):
    half = rows.shape[1] // 2
    return jnp.concatenate([rows[:, :half], rows[:, half:]], axis=0)


def unfolded(piece):
    return jnp.concatenate([piece[:8], piece[8:]], axis=1)


def place_of(step):
    return (step - 2) % NZ


def beside(shape, base):
    r = lax.broadcasted_iota(jnp.int32, shape, 0)
    lane = lax.broadcasted_iota(jnp.int32, shape, 1) - base
    return lane == lax.rem(r + 1, 8), lane == lax.rem(r + 2, 8)


def two_terms(value):
    high = value.astype(BF16).astype(F32)
    return high, value - high


def place(rows, base, grad):
    one, two = beside(rows.shape, base)
    high, low = two_terms(grad)
    return jnp.where(one, high, jnp.where(two, low, rows))


def split_again(rows, base):
    one, two = beside(rows.shape, base)
    high, low = two_terms(jnp.sum(jnp.where(one | two, rows, 0.0), axis=0, keepdims=True))
    return jnp.where(one, high, jnp.where(two, low, rows))


def in_tiles(rows, first, change):
    if first < 0 or first * 128 >= rows.shape[1]:
        return rows
    low, high = first * 128, first * 128 + 256
    parts = [rows[:, :low], change(rows[:, low:high]), rows[:, high:]]
    return jnp.concatenate([part for part in parts if part.shape[1]], axis=1)


def kernel(
    jac, mis_in, taps_in, rows_out,
    mis, taps, xbuf, white, white_t, wm_rows, mis_tail, acc,
    keep_a, keep_b, core_sa, core_sb, core_ra, core_rb,
    s1a, s1b, r1a, r1b, a2, b2, s2a, s2b, r2a, r2b,
    load_sem, halo_ss, halo_rs, core_ss, core_rs,
    s1a_ss, s1a_rs, s1b_ss, s1b_rs, s2a_ss, s2a_rs, s2b_ss, s2b_rs,
):
    me = lax.axis_index("tm")
    x, z, y, c = me // (NZ * NY * NC), (me // (NY * NC)) % NZ, (me // NC) % NY, me % NC
    sibling = position(x, z, y, c + 1)
    after, before = lax.rem(me + 1, OWNERS), lax.rem(me + OWNERS - 1, OWNERS)
    xy_dev = [position(x + dx, z, y + dy, c) for dx, dy in XY_STEPS]
    xy_own = [lax.rem(x + dx, NX) * NY + lax.rem(y + dy, NY) for dx, dy in XY_STEPS]
    z_dev = [position(x, z + dz, y, c) for dz in Z_STEPS]
    z_own = [lax.rem(z + dz, NZ) for dz in Z_STEPS]
    u = x * NY + y
    z_place = [lax.rem(zo + 2 * NZ - z - 2, NZ) for zo in range(NZ)]
    z_rows = [p // NP * 512 + p % NP * 32 for p in z_place]
    z_at = [lax.rem(z + 2 + p, NZ) for p in range(NZ)]

    loads = []
    for i, (low, high) in enumerate(zip(BOUNDS[:-1], BOUNDS[1:])):
        loads.append(pltpu.make_async_copy(
            jac.at[pl.ds(low, high - low)], xbuf.at[pl.ds(ORDER + low, high - low)], load_sem.at[i]
        ))

    small = [
        pltpu.make_async_copy(taps_in, taps, load_sem.at[CHUNKS]),
        pltpu.make_async_copy(mis_in, mis, load_sem.at[CHUNKS + 1]),
    ]
    for load in small + loads[::-1]:
        load.start()

    barrier = pltpu.get_barrier_semaphore()
    partners = [sibling, after, before] + xy_dev + z_dev
    for device in partners:
        pl.semaphore_signal(barrier, inc=1, device_id={"tm": device}, device_id_type=MESH)

    for load in small:
        load.wait()

    coef = jnp.broadcast_to(taps[...].astype(BF16), (16, ORDER))
    lag_of = lax.broadcasted_iota(jnp.int32, (ORDER, 256), 0)
    lane_of = lax.broadcasted_iota(jnp.int32, (ORDER, 256), 1)
    flip = (lag_of + lane_of == ORDER - 1).astype(F32).astype(BF16)
    first = jnp.dot(coef, flip, preferred_element_type=F32)[:1]
    lane = lax.broadcasted_iota(jnp.int32, (1, 256), 1)
    first = jnp.where(lane == ORDER, 1.0, -first)
    matrix = pltpu.roll(jnp.broadcast_to(first, (BLOCK, 256)), 0, 1, stride=1, stride_axis=0).astype(BF16)
    mis_matrix = pltpu.roll(jnp.broadcast_to(first, (128, 256)), ORDER, 1, stride=1, stride_axis=0).astype(BF16)

    def whiten_misfit(tail):
        here = mis[...].astype(F32)
        row_of = lax.broadcasted_iota(jnp.int32, (16, 128), 0)
        previous = jnp.where(row_of == 0, pltpu.roll(tail, 1, 0), pltpu.roll(here, 1, 0))
        both = jnp.concatenate([previous, here], axis=1).astype(BF16)
        return lax.dot_general(both, mis_matrix, (((1,), (1,)), ((), ())), preferred_element_type=F32)

    def put_misfit(white_mis, i):
        wm_rows[:, i * 128 : (i + 1) * 128] = jnp.broadcast_to(white_mis[i : i + 1], (16, 128)).astype(BF16)

    white_mis = whiten_misfit(jnp.zeros((16, 128), F32))
    for i in range(1, 16):
        put_misfit(white_mis, i)

    def whiten(start, rows):
        out = jnp.dot(
            matrix[:rows, : rows + ORDER], xbuf[start : start + rows + ORDER], preferred_element_type=F32
        )
        white[start : start + rows] = out.astype(BF16)

    def transpose(i):
        block = white[i * KROWS : (i + 1) * KROWS].T
        for zo in range(NZ):
            for xo in range(NX):
                pass
        white_t[:, i * KROWS : (i + 1) * KROWS] = block

    halo = pltpu.make_async_remote_copy(
        src_ref=jac.at[pl.ds(ROWS - ORDER, ORDER)], dst_ref=xbuf.at[pl.ds(0, ORDER)],
        send_sem=halo_ss.at[0], recv_sem=halo_rs.at[0], device_id={"tm": after}, device_id_type=MESH,
    )
    mis_halo = pltpu.make_async_remote_copy(
        src_ref=mis_in, dst_ref=mis_tail,
        send_sem=halo_ss.at[1], recv_sem=halo_rs.at[1], device_id={"tm": after}, device_id_type=MESH,
    )

    ready, turned = CHUNKS, ROWS // KROWS
    for start in list(range(0, ROWS, BLOCK))[:0:-1]:
        rows = min(BLOCK, ROWS - start)
        while BOUNDS[ready] > start - ORDER:
            ready -= 1
            loads[ready].wait()
        if start == GREET * BLOCK:
            pl.semaphore_wait(barrier, len(partners))

            @pl.when(me < OWNERS - 1)
            def _():
                halo.start()
                mis_halo.start()

        whiten(start, rows)
        while (turned - 1) * KROWS >= start:
            turned -= 1
            transpose(turned)
    while ready > 0:
        ready -= 1
        loads[ready].wait()

    def z_group(row):
        half, xo, pp = row // 512, row // 128 % NX, row // 32 % NP
        return pl.ds(pl.multiple_of(xo * 256 + z_at[half * NP + pp] * 32, 32), 32)

    def product(row, rows, left, right, low, high):
        parts = []
        for i in range(row, row + rows, MROWS):
            lhs = jnp.concatenate(
                [white_t[z_group(j), low:high] for j in range(i, i + MROWS, 32)], axis=0
            )
            if i + MROWS == row + rows:
                lhs = jnp.concatenate([lhs, wm_rows[:, low:high]], axis=0)
            parts.append(jnp.dot(lhs, white[low:high, left:right], preferred_element_type=F32))
        return jnp.concatenate(parts, axis=0)

    def gram_a(low, high):
        return product(0, WIDTH, 0, ACOLS, low, high)

    def gram_b(half, low, high):
        return product(half * 512, 512, ACOLS, WIDTH, low, high)

    acc[...] = gram_b(0, KROWS, ROWS)

    @pl.when(me > 0)
    def _():
        halo.wait_recv()
        mis_halo.wait_recv()

    @pl.when(me == 0)
    def _():
        xbuf[:ORDER] = jnp.zeros((ORDER, WIDTH), BF16)
        mis_tail[...] = jnp.zeros_like(mis_tail)

    whiten(0, BLOCK)
    transpose(0)
    put_misfit(whiten_misfit(mis_tail[...].astype(F32)), 0)

    def to_sibling(src, dst, k):
        return pltpu.make_async_remote_copy(
            src_ref=src, dst_ref=dst, send_sem=core_ss.at[k], recv_sem=core_rs.at[k],
            device_id={"tm": sibling}, device_id_type=MESH,
        )

    mine_first = c == 0

    def base_of(p, yo, side):
        return z_at[p] * 32 + (yo * NC + side) * 8

    def deal(rows, grad, first, p, yo, keep, send, index):
        pair = []
        for side in range(NC):
            part = rows[side * 8 : side * 8 + 8]

            def change(tiles, side=side):
                return place(tiles, base_of(p, yo, side), grad[:, first * 128 : first * 128 + 256])

            pair.append(folded(in_tiles(part, first, change)))
        keep[index] = jnp.where(mine_first, pair[0], pair[1])
        send[index] = jnp.where(mine_first, pair[1], pair[0]).astype(BF16)

    def both_cores(keep, received, index, first, p, yo):
        rows = keep[index] + received[index].astype(F32)
        if first < 0 or first * 128 >= 2 * rows.shape[1]:
            return rows.astype(BF16)
        rows = in_tiles(unfolded(rows), first, lambda tiles: split_again(tiles, base_of(p, yo, c)))
        return folded(rows).astype(BF16)

    stage1a, stage1b, core_b = [], [], []

    def finish_b(half, out):
        for xo in range(NX):
            for pp in range(NP):
                for yo in range(NY):
                    row = xo * 128 + pp * 32 + yo * 16
                    deal(
                        out[row : row + 16], out[512:513], xo * 2 - 2, half * NP + pp, yo,
                        keep_b, core_sb, (half * NU + xo * NY + yo) * NP + pp,
                    )
        span = pl.ds(half * NU * NP, NU * NP)
        copy = to_sibling(core_sb.at[span], core_rb.at[span], 1 + half)
        copy.start()
        core_b.append(copy)

    def send_b(half):
        core_b[half].wait_recv()
        for xo in range(NX):
            for yo in range(NY):
                for pp in range(NP):
                    index = (half * NU + xo * NY + yo) * NP + pp
                    s1b[index] = both_cores(keep_b, core_rb, index, xo * 2 - 2, half * NP + pp, yo)
        for k, (device, own) in enumerate(zip(xy_dev, xy_own)):
            copy = pltpu.make_async_remote_copy(
                src_ref=s1b.at[pl.ds((half * NU + own) * NP, NP)], dst_ref=r1b.at[half, k],
                send_sem=s1b_ss.at[half * 7 + k], recv_sem=s1b_rs.at[half * 7 + k],
                device_id={"tm": device}, device_id_type=MESH,
            )
            copy.start()
            stage1b.append(copy)

    finish_b(0, acc[...] + gram_b(0, 0, KROWS))

    out = gram_a(0, ROWS)
    for half in range(HALVES):
        for xo in range(NX):
            for pp in range(NP):
                for yo in range(NY):
                    row = half * 512 + xo * 128 + pp * 32 + yo * 16
                    p = half * NP + pp
                    deal(
                        out[row : row + 16], out[WIDTH : WIDTH + 1], xo * 2, p, yo,
                        keep_a, core_sa, p * NU + xo * NY + yo,
                    )
    core_a = to_sibling(core_sa, core_ra, 0)
    core_a.start()
    send_b(0)

    finish_b(1, gram_b(1, 0, ROWS))

    core_a.wait_recv()
    for p in range(NZ):
        for xo in range(NX):
            for yo in range(NY):
                index = p * NU + xo * NY + yo
                s1a[index] = both_cores(keep_a, core_ra, index, xo * 2, p, yo)
    for k, (device, step) in enumerate(zip(z_dev, Z_STEPS)):
        copy = pltpu.make_async_remote_copy(
            src_ref=s1a.at[pl.ds(place_of(step) * NU, NU)], dst_ref=r1a.at[k],
            send_sem=s1a_ss.at[k], recv_sem=s1a_rs.at[k], device_id={"tm": device}, device_id_type=MESH,
        )
        copy.start()
        stage1a.append(copy)
    send_b(1)

    stage2b = {}

    def pass_b(half):
        span = pl.ds((half * NU + u) * NP, NP)
        b2[half] = keep_b[span] + core_rb[span].astype(F32)
        for k in range(7):
            stage1b[half * 7 + k].wait_recv()
            b2[half] += r1b[half, k].astype(F32)
        for pp in range(NP):
            p = half * NP + pp
            lane = x * 256 - ACOLS + base_of(p, y, c)
            s2b[p] = folded(split_again(unfolded(b2[half, pp]), lane)).astype(BF16)
        for k, (device, step) in enumerate(zip(z_dev, Z_STEPS)):
            p = place_of(step)
            if p // NP == half:
                copy = pltpu.make_async_remote_copy(
                    src_ref=s2b.at[p], dst_ref=r2b.at[k],
                    send_sem=s2b_ss.at[k], recv_sem=s2b_rs.at[k], device_id={"tm": device}, device_id_type=MESH,
                )
                copy.start()
                stage2b[k] = copy

    pass_b(0)

    span = pl.ds(place_of(0) * NU, NU)
    a2[...] = keep_a[span] + core_ra[span].astype(F32)
    for k, copy in enumerate(stage1a):
        copy.wait_recv()
        a2[...] += r1a[k].astype(F32)
    for xo in range(NX):
        for yo in range(NY):
            rows = a2[xo * NY + yo]
            if xo == 0:
                rows = folded(split_again(unfolded(rows), base_of(place_of(0), yo, c)))
            s2a[xo * NY + yo] = rows.astype(BF16)
    stage2a = []
    for k, (device, own) in enumerate(zip(xy_dev, xy_own)):
        copy = pltpu.make_async_remote_copy(
            src_ref=s2a.at[own], dst_ref=r2a.at[k],
            send_sem=s2a_ss.at[k], recv_sem=s2a_rs.at[k], device_id={"tm": device}, device_id_type=MESH,
        )
        copy.start()
        stage2a.append(copy)

    pass_b(1)

    last_a, last_b = a2[u], b2[place_of(0) // NP, place_of(0) % NP]
    for k, copy in enumerate(stage2a):
        copy.wait_recv()
        last_a = last_a + r2a[k].astype(F32)

    @pl.when(me < OWNERS - 1)
    def _():
        halo.wait_send()
        mis_halo.wait_send()

    for copy in [core_a] + core_b + stage1a + stage1b + stage2a:
        copy.wait_send()

    for k, copy in stage2b.items():
        copy.wait_recv()
        last_b = last_b + r2b[k].astype(F32)
    rows_out[:, :ACOLS] = unfolded(last_a)
    rows_out[:, ACOLS:] = unfolded(last_b)

    for copy in stage2b.values():
        copy.wait_send()


def outputs(rows_ref, fisher, newton):
    rows = rows_ref[...]
    r = lax.broadcasted_iota(jnp.int32, rows.shape, 0)
    col = lax.broadcasted_iota(jnp.int32, rows.shape, 1) - lax.axis_index("tm") * 8
    one, two, on = col == lax.rem(r + 1, 8), col == lax.rem(r + 2, 8), col == r

    def picked(mask, values):
        return jnp.broadcast_to(jnp.sum(jnp.where(mask, values, 0.0), axis=1, keepdims=True), (8, 128))

    grad = pltpu.roll(picked(one, rows), 1, 0) + pltpu.roll(picked(two, rows), 2, 0)
    diagonal = picked(on, rows)
    mirror_one = picked(on, pltpu.roll(rows, 7, 0))[:, :1]
    mirror_two = picked(on, pltpu.roll(rows, 6, 0))[:, :1]
    fisher[...] = jnp.where(one, mirror_one, jnp.where(two, mirror_two, rows)) * (1.0 / TOTAL)
    r8 = lax.broadcasted_iota(jnp.int32, (8, 128), 0)
    c8 = lax.broadcasted_iota(jnp.int32, (8, 128), 1)
    newton[...] = jnp.sum(jnp.where(r8 == c8, grad / diagonal, 0.0), axis=0, keepdims=True)[:, :8]


def shards(jacobian, misfit, taps):
    dma = pltpu.SemaphoreType.DMA
    vmem = pl.BlockSpec(memory_space=pltpu.VMEM)
    rows = pl.pallas_call(
        kernel,
        out_shape=pltpu.VMEM((8, WIDTH), F32),
        in_specs=[pl.BlockSpec(memory_space=pl.ANY)] * 3,
        out_specs=vmem,
        scratch_shapes=[
            pltpu.VMEM((16, 128), BF16),
            pltpu.VMEM((1, ORDER), F32),
            pltpu.VMEM((ROWS + ORDER, WIDTH), BF16),
            pltpu.VMEM((ROWS, WIDTH), BF16),
            pltpu.VMEM((WIDTH, ROWS), BF16),
            pltpu.VMEM((16, ROWS), BF16),
            pltpu.VMEM((16, 128), BF16),
            pltpu.VMEM((512 + 16, BCOLS), F32),
            pltpu.VMEM((64, 16, AHALF), F32),
            pltpu.VMEM((64, 16, BHALF), F32),
            pltpu.VMEM((64, 16, AHALF), BF16),
            pltpu.VMEM((64, 16, BHALF), BF16),
            pltpu.VMEM((64, 16, AHALF), BF16),
            pltpu.VMEM((64, 16, BHALF), BF16),
            pltpu.VMEM((64, 16, AHALF), BF16),
            pltpu.VMEM((64, 16, BHALF), BF16),
            pltpu.VMEM((7, 8, 16, AHALF), BF16),
            pltpu.VMEM((HALVES, 7, NP, 16, BHALF), BF16),
            pltpu.VMEM((8, 16, AHALF), F32),
            pltpu.VMEM((HALVES, NP, 16, BHALF), F32),
            pltpu.VMEM((8, 16, AHALF), BF16),
            pltpu.VMEM((8, 16, BHALF), BF16),
            pltpu.VMEM((7, 16, AHALF), BF16),
            pltpu.VMEM((7, 16, BHALF), BF16),
            dma((CHUNKS + 2,)), dma((2,)), dma((2,)), dma((3,)), dma((3,)),
            dma((7,)), dma((7,)), dma((14,)), dma((14,)), dma((7,)), dma((7,)), dma((7,)), dma((7,)),
        ],
        compiler_params=pltpu.CompilerParams(
            collective_id=0, has_side_effects=True, vmem_limit_bytes=56 * 1024 * 1024
        ),
    )(jacobian, misfit.reshape(16, 128), taps.reshape(1, ORDER))
    fisher, newton = pl.pallas_call(
        outputs,
        out_shape=(jax.ShapeDtypeStruct((8, WIDTH), F32), jax.ShapeDtypeStruct((1, 8), F32)),
        in_specs=[vmem],
        out_specs=(vmem, vmem),
    )(pltpu.with_memory_space_constraint(rows, pltpu.VMEM))
    return fisher, newton.reshape(8)


def solution(mesh):
    in_specs = (P(("net", "tm"), None), P(("net", "tm")), P("net"))
    out_specs = (P(("net", "tm"), None), P(("net", "tm")))
    return jax.shard_map(shards, mesh=mesh, in_specs=in_specs, out_specs=out_specs, check_vma=False)
```

```python
import jax
import jax.numpy as jnp
from jax import lax
from jax.experimental import pallas as pl
from jax.experimental.pallas import tpu as pltpu
from jax.sharding import PartitionSpec as P

NX, NZ, NY, NC = 4, 8, 2, 2
NU = NX * NY
OWNERS = NX * NZ * NY * NC
MESH = pl.DeviceIdType.MESH
BF16, F32 = jnp.bfloat16, jnp.float32

ROWS, WIDTH, ORDER = 2048, 1024, 64
BLOCK = 192
GREET = 8
BOUNDS = [0, 512, 1024, 1536, 2048]
CHUNKS = len(BOUNDS) - 1
KROWS = 256
MROWS = 256
ACOLS = 256
BCOLS = WIDTH - ACOLS
AHALF, BHALF = ACOLS // 2, BCOLS // 2
TOTAL = ROWS * OWNERS
XY_STEPS = [(0, 1), (2, 1), (1, 1), (3, 1), (2, 0), (1, 0), (3, 0)]
Z_STEPS = [4, 3, 5, 2, 6, 1, 7]
GROUPS = [(0, 4), (4, 8)]
PLAN = [("gram", "a"), ("send", 0), ("send", "a"), ("gram", 1), ("send", 1)]
PASSES = [0, "a", 1]


def position(x, z, y, c):
    return ((lax.rem(x, NX) * NZ + lax.rem(z, NZ)) * NY + lax.rem(y, NY)) * NC + lax.rem(c, NC)


def folded(rows):
    half = rows.shape[1] // 2
    return jnp.concatenate([rows[:, :half], rows[:, half:]], axis=0)


def unfolded(piece):
    return jnp.concatenate([piece[:8], piece[8:]], axis=1)


def place_of(step):
    return (step - 2) % NZ


def beside(shape, base):
    r = lax.broadcasted_iota(jnp.int32, shape, 0)
    lane = lax.broadcasted_iota(jnp.int32, shape, 1) - base
    return lane == lax.rem(r + 1, 8), lane == lax.rem(r + 2, 8)


def two_terms(value):
    high = value.astype(BF16).astype(F32)
    return high, value - high


def place(rows, base, grad):
    one, two = beside(rows.shape, base)
    high, low = two_terms(grad)
    return jnp.where(one, high, jnp.where(two, low, rows))


def split_again(rows, base):
    one, two = beside(rows.shape, base)
    high, low = two_terms(jnp.sum(jnp.where(one | two, rows, 0.0), axis=0, keepdims=True))
    return jnp.where(one, high, jnp.where(two, low, rows))


def in_tiles(rows, first, change):
    if first < 0 or first * 128 >= rows.shape[1]:
        return rows
    low, high = first * 128, first * 128 + 256
    parts = [rows[:, :low], change(rows[:, low:high]), rows[:, high:]]
    return jnp.concatenate([part for part in parts if part.shape[1]], axis=1)


def kernel(
    jac, mis_in, taps_in, rows_out,
    mis, taps, xbuf, white, white_t, wm_rows, mis_tail, acc,
    keep_a, keep_b, core_sa, core_sb, core_ra, core_rb,
    s1a, s1b, r1a, r1b, a2, b2, s2a, s2b, r2a, r2b,
    load_sem, halo_ss, halo_rs, core_ss, core_rs,
    s1a_ss, s1a_rs, s1b_ss, s1b_rs, s2a_ss, s2a_rs, s2b_ss, s2b_rs,
):
    me = lax.axis_index("tm")
    x, z, y, c = me // (NZ * NY * NC), (me // (NY * NC)) % NZ, (me // NC) % NY, me % NC
    sibling = position(x, z, y, c + 1)
    after, before = lax.rem(me + 1, OWNERS), lax.rem(me + OWNERS - 1, OWNERS)
    xy_dev = [position(x + dx, z, y + dy, c) for dx, dy in XY_STEPS]
    xy_own = [lax.rem(x + dx, NX) * NY + lax.rem(y + dy, NY) for dx, dy in XY_STEPS]
    z_dev = [position(x, z + dz, y, c) for dz in Z_STEPS]
    z_own = [lax.rem(z + dz, NZ) for dz in Z_STEPS]
    u = x * NY + y
    z_at = [lax.rem(z + 2 + p, NZ) for p in range(NZ)]

    loads = []
    for i, (low, high) in enumerate(zip(BOUNDS[:-1], BOUNDS[1:])):
        loads.append(pltpu.make_async_copy(
            jac.at[pl.ds(low, high - low)], xbuf.at[pl.ds(ORDER + low, high - low)], load_sem.at[i]
        ))

    small = [
        pltpu.make_async_copy(taps_in, taps, load_sem.at[CHUNKS]),
        pltpu.make_async_copy(mis_in, mis, load_sem.at[CHUNKS + 1]),
    ]
    for load in small + loads[::-1]:
        load.start()

    barrier = pltpu.get_barrier_semaphore()
    partners = [sibling, after, before] + xy_dev + z_dev
    for device in partners:
        pl.semaphore_signal(barrier, inc=1, device_id={"tm": device}, device_id_type=MESH)

    for load in small:
        load.wait()

    coef = jnp.broadcast_to(taps[...].astype(BF16), (16, ORDER))
    lag_of = lax.broadcasted_iota(jnp.int32, (ORDER, 256), 0)
    lane_of = lax.broadcasted_iota(jnp.int32, (ORDER, 256), 1)
    flip = (lag_of + lane_of == ORDER - 1).astype(F32).astype(BF16)
    first = jnp.dot(coef, flip, preferred_element_type=F32)[:1]
    lane = lax.broadcasted_iota(jnp.int32, (1, 256), 1)
    first = jnp.where(lane == ORDER, 1.0, -first)
    matrix = pltpu.roll(jnp.broadcast_to(first, (BLOCK, 256)), 0, 1, stride=1, stride_axis=0).astype(BF16)
    mis_matrix = pltpu.roll(jnp.broadcast_to(first, (128, 256)), ORDER, 1, stride=1, stride_axis=0).astype(BF16)

    def whiten_misfit(tail):
        here = mis[...].astype(F32)
        row_of = lax.broadcasted_iota(jnp.int32, (16, 128), 0)
        previous = jnp.where(row_of == 0, pltpu.roll(tail, 1, 0), pltpu.roll(here, 1, 0))
        both = jnp.concatenate([previous, here], axis=1).astype(BF16)
        return lax.dot_general(both, mis_matrix, (((1,), (1,)), ((), ())), preferred_element_type=F32)

    def put_misfit(white_mis, i):
        wm_rows[:, i * 128 : (i + 1) * 128] = jnp.broadcast_to(white_mis[i : i + 1], (16, 128)).astype(BF16)

    white_mis = whiten_misfit(jnp.zeros((16, 128), F32))
    for i in range(1, 16):
        put_misfit(white_mis, i)

    def whiten(start, rows):
        out = jnp.dot(
            matrix[:rows, : rows + ORDER], xbuf[start : start + rows + ORDER], preferred_element_type=F32
        )
        white[start : start + rows] = out.astype(BF16)

    def transpose(i):
        block = white[i * KROWS : (i + 1) * KROWS].T
        for zo in range(NZ):
            for xo in range(NX):
                pass
        white_t[:, i * KROWS : (i + 1) * KROWS] = block

    halo = pltpu.make_async_remote_copy(
        src_ref=jac.at[pl.ds(ROWS - ORDER, ORDER)], dst_ref=xbuf.at[pl.ds(0, ORDER)],
        send_sem=halo_ss.at[0], recv_sem=halo_rs.at[0], device_id={"tm": after}, device_id_type=MESH,
    )
    mis_halo = pltpu.make_async_remote_copy(
        src_ref=mis_in, dst_ref=mis_tail,
        send_sem=halo_ss.at[1], recv_sem=halo_rs.at[1], device_id={"tm": after}, device_id_type=MESH,
    )

    ready, turned = CHUNKS, ROWS // KROWS
    for start in list(range(0, ROWS, BLOCK))[:0:-1]:
        rows = min(BLOCK, ROWS - start)
        while BOUNDS[ready] > start - ORDER:
            ready -= 1
            loads[ready].wait()
        if start == GREET * BLOCK:
            pl.semaphore_wait(barrier, len(partners))

            @pl.when(me < OWNERS - 1)
            def _():
                halo.start()
                mis_halo.start()

        whiten(start, rows)
        while (turned - 1) * KROWS >= start:
            turned -= 1
            transpose(turned)
    while ready > 0:
        ready -= 1
        loads[ready].wait()

    def z_group(low, high, row):
        xo, p = row // ((high - low) * 32), low + row // 32 % (high - low)
        return pl.ds(pl.multiple_of(xo * 256 + z_at[p] * 32, 32), 32)

    def product(group, left, right, first, last):
        low, high = group
        rows, parts = NX * (high - low) * 32, []
        for i in range(0, rows, MROWS):
            lhs = [white_t[z_group(low, high, j), first:last] for j in range(i, i + MROWS, 32)]
            if i + MROWS == rows:
                lhs.append(wm_rows[:, first:last])
            lhs = jnp.concatenate(lhs, axis=0)
            parts.append(jnp.dot(lhs, white[first:last, left:right], preferred_element_type=F32))
        return jnp.concatenate(parts, axis=0)

    def gram_a(first, last):
        return product((0, NZ), 0, ACOLS, first, last)

    def gram_b(g, first, last):
        return product(GROUPS[g], ACOLS, WIDTH, first, last)

    acc[...] = gram_b(0, KROWS, ROWS)

    @pl.when(me > 0)
    def _():
        halo.wait_recv()
        mis_halo.wait_recv()

    @pl.when(me == 0)
    def _():
        xbuf[:ORDER] = jnp.zeros((ORDER, WIDTH), BF16)
        mis_tail[...] = jnp.zeros_like(mis_tail)

    whiten(0, BLOCK)
    transpose(0)
    put_misfit(whiten_misfit(mis_tail[...].astype(F32)), 0)

    def to_sibling(src, dst, k):
        return pltpu.make_async_remote_copy(
            src_ref=src, dst_ref=dst, send_sem=core_ss.at[k], recv_sem=core_rs.at[k],
            device_id={"tm": sibling}, device_id_type=MESH,
        )

    mine_first = c == 0

    def base_of(p, yo, side):
        return z_at[p] * 32 + (yo * NC + side) * 8

    def deal(rows, grad, first, p, yo, keep, send, index):
        pair = []
        for side in range(NC):
            part = rows[side * 8 : side * 8 + 8]

            def change(tiles, side=side):
                return place(tiles, base_of(p, yo, side), grad[:, first * 128 : first * 128 + 256])

            pair.append(folded(in_tiles(part, first, change)))
        keep[index] = jnp.where(mine_first, pair[0], pair[1])
        send[index] = jnp.where(mine_first, pair[1], pair[0]).astype(BF16)

    def both_cores(keep, received, index, first, p, yo):
        rows = keep[index] + received[index].astype(F32)
        if first < 0 or first * 128 >= 2 * rows.shape[1]:
            return rows.astype(BF16)
        rows = in_tiles(unfolded(rows), first, lambda tiles: split_again(tiles, base_of(p, yo, c)))
        return folded(rows).astype(BF16)

    stage1a, stage1b, stage2a, stage2b, core = [], {}, [], {}, {}

    def slot(g, own, p):
        low, high = GROUPS[g]
        return low * NU + own * (high - low) + p - low

    def finish_b(g, out):
        low, high = GROUPS[g]
        row = 0
        for xo in range(NX):
            for p in range(low, high):
                for yo in range(NY):
                    deal(
                        out[row : row + 16], out[-16:-15], xo * 2 - 2, p, yo,
                        keep_b, core_sb, slot(g, xo * NY + yo, p),
                    )
                    row += 16
        span = pl.ds(low * NU, (high - low) * NU)
        core[g] = to_sibling(core_sb.at[span], core_rb.at[span], 1 + g)
        core[g].start()

    def send_b(g):
        low, high = GROUPS[g]
        core[g].wait_recv()
        for xo in range(NX):
            for yo in range(NY):
                for p in range(low, high):
                    index = slot(g, xo * NY + yo, p)
                    s1b[index] = both_cores(keep_b, core_rb, index, xo * 2 - 2, p, yo)
        for k, (device, own) in enumerate(zip(xy_dev, xy_own)):
            copy = pltpu.make_async_remote_copy(
                src_ref=s1b.at[pl.ds(slot(g, own, low), high - low)], dst_ref=r1b.at[k, low:high],
                send_sem=s1b_ss.at[g * 7 + k], recv_sem=s1b_rs.at[g * 7 + k],
                device_id={"tm": device}, device_id_type=MESH,
            )
            copy.start()
            stage1b[g, k] = copy

    def finish_a(out):
        row = 0
        for xo in range(NX):
            for p in range(NZ):
                for yo in range(NY):
                    deal(
                        out[row : row + 16], out[WIDTH : WIDTH + 1], xo * 2, p, yo,
                        keep_a, core_sa, p * NU + xo * NY + yo,
                    )
                    row += 16
        core["a"] = to_sibling(core_sa, core_ra, 0)
        core["a"].start()

    def send_a():
        core["a"].wait_recv()
        for p in range(NZ):
            for xo in range(NX):
                for yo in range(NY):
                    index = p * NU + xo * NY + yo
                    s1a[index] = both_cores(keep_a, core_ra, index, xo * 2, p, yo)
        for k, (device, step) in enumerate(zip(z_dev, Z_STEPS)):
            copy = pltpu.make_async_remote_copy(
                src_ref=s1a.at[pl.ds(place_of(step) * NU, NU)], dst_ref=r1a.at[k],
                send_sem=s1a_ss.at[k], recv_sem=s1a_rs.at[k], device_id={"tm": device}, device_id_type=MESH,
            )
            copy.start()
            stage1a.append(copy)

    def send(item):
        if item == "a":
            send_a()
        else:
            send_b(item)

    finish_b(0, acc[...] + gram_b(0, 0, KROWS))
    for act, item in PLAN:
        if act == "send":
            send(item)
        elif item == "a":
            finish_a(gram_a(0, ROWS))
        else:
            finish_b(item, gram_b(item, 0, ROWS))

    def pass_b(g):
        low, high = GROUPS[g]
        span = pl.ds(slot(g, u, low), high - low)
        b2[low:high] = keep_b[span] + core_rb[span].astype(F32)
        for k in range(7):
            stage1b[g, k].wait_recv()
            b2[low:high] += r1b[k, low:high].astype(F32)
        for p in range(low, high):
            lane = x * 256 - ACOLS + base_of(p, y, c)
            s2b[p] = folded(split_again(unfolded(b2[p]), lane)).astype(BF16)
        for k, (device, step) in enumerate(zip(z_dev, Z_STEPS)):
            p = place_of(step)
            if low <= p < high:
                copy = pltpu.make_async_remote_copy(
                    src_ref=s2b.at[p], dst_ref=r2b.at[k],
                    send_sem=s2b_ss.at[k], recv_sem=s2b_rs.at[k], device_id={"tm": device}, device_id_type=MESH,
                )
                copy.start()
                stage2b[k] = copy

    def pass_a():
        span = pl.ds(place_of(0) * NU, NU)
        a2[...] = keep_a[span] + core_ra[span].astype(F32)
        for k, copy in enumerate(stage1a):
            copy.wait_recv()
            a2[...] += r1a[k].astype(F32)
        for xo in range(NX):
            for yo in range(NY):
                rows = a2[xo * NY + yo]
                if xo == 0:
                    rows = folded(split_again(unfolded(rows), base_of(place_of(0), yo, c)))
                s2a[xo * NY + yo] = rows.astype(BF16)
        for k, (device, own) in enumerate(zip(xy_dev, xy_own)):
            copy = pltpu.make_async_remote_copy(
                src_ref=s2a.at[own], dst_ref=r2a.at[k],
                send_sem=s2a_ss.at[k], recv_sem=s2a_rs.at[k], device_id={"tm": device}, device_id_type=MESH,
            )
            copy.start()
            stage2a.append(copy)

    for item in PASSES:
        if item == "a":
            pass_a()
        else:
            pass_b(item)

    last_a, last_b = a2[u], b2[place_of(0)]
    for k, copy in enumerate(stage2a):
        copy.wait_recv()
        last_a = last_a + r2a[k].astype(F32)

    @pl.when(me < OWNERS - 1)
    def _():
        halo.wait_send()
        mis_halo.wait_send()

    for copy in list(core.values()) + stage1a + list(stage1b.values()) + stage2a:
        copy.wait_send()

    for k, copy in stage2b.items():
        copy.wait_recv()
        last_b = last_b + r2b[k].astype(F32)
    rows_out[:, :ACOLS] = unfolded(last_a)
    rows_out[:, ACOLS:] = unfolded(last_b)

    for copy in stage2b.values():
        copy.wait_send()


def outputs(rows_ref, fisher, newton):
    rows = rows_ref[...]
    r = lax.broadcasted_iota(jnp.int32, rows.shape, 0)
    col = lax.broadcasted_iota(jnp.int32, rows.shape, 1) - lax.axis_index("tm") * 8
    one, two, on = col == lax.rem(r + 1, 8), col == lax.rem(r + 2, 8), col == r

    def picked(mask, values):
        return jnp.broadcast_to(jnp.sum(jnp.where(mask, values, 0.0), axis=1, keepdims=True), (8, 128))

    grad = pltpu.roll(picked(one, rows), 1, 0) + pltpu.roll(picked(two, rows), 2, 0)
    diagonal = picked(on, rows)
    mirror_one = picked(on, pltpu.roll(rows, 7, 0))[:, :1]
    mirror_two = picked(on, pltpu.roll(rows, 6, 0))[:, :1]
    fisher[...] = jnp.where(one, mirror_one, jnp.where(two, mirror_two, rows)) * (1.0 / TOTAL)
    r8 = lax.broadcasted_iota(jnp.int32, (8, 128), 0)
    c8 = lax.broadcasted_iota(jnp.int32, (8, 128), 1)
    newton[...] = jnp.sum(jnp.where(r8 == c8, grad / diagonal, 0.0), axis=0, keepdims=True)[:, :8]


def shards(jacobian, misfit, taps):
    dma = pltpu.SemaphoreType.DMA
    vmem = pl.BlockSpec(memory_space=pltpu.VMEM)
    rows = pl.pallas_call(
        kernel,
        out_shape=pltpu.VMEM((8, WIDTH), F32),
        in_specs=[pl.BlockSpec(memory_space=pl.ANY)] * 3,
        out_specs=vmem,
        scratch_shapes=[
            pltpu.VMEM((16, 128), BF16),
            pltpu.VMEM((1, ORDER), F32),
            pltpu.VMEM((ROWS + ORDER, WIDTH), BF16),
            pltpu.VMEM((ROWS, WIDTH), BF16),
            pltpu.VMEM((WIDTH, ROWS), BF16),
            pltpu.VMEM((16, ROWS), BF16),
            pltpu.VMEM((16, 128), BF16),
            pltpu.VMEM((NX * (GROUPS[0][1] - GROUPS[0][0]) * 32 + 16, BCOLS), F32),
            pltpu.VMEM((64, 16, AHALF), F32),
            pltpu.VMEM((64, 16, BHALF), F32),
            pltpu.VMEM((64, 16, AHALF), BF16),
            pltpu.VMEM((64, 16, BHALF), BF16),
            pltpu.VMEM((64, 16, AHALF), BF16),
            pltpu.VMEM((64, 16, BHALF), BF16),
            pltpu.VMEM((64, 16, AHALF), BF16),
            pltpu.VMEM((64, 16, BHALF), BF16),
            pltpu.VMEM((7, 8, 16, AHALF), BF16),
            pltpu.VMEM((7, NZ, 16, BHALF), BF16),
            pltpu.VMEM((8, 16, AHALF), F32),
            pltpu.VMEM((NZ, 16, BHALF), F32),
            pltpu.VMEM((8, 16, AHALF), BF16),
            pltpu.VMEM((8, 16, BHALF), BF16),
            pltpu.VMEM((7, 16, AHALF), BF16),
            pltpu.VMEM((7, 16, BHALF), BF16),
            dma((CHUNKS + 2,)), dma((2,)), dma((2,)), dma((len(GROUPS) + 1,)), dma((len(GROUPS) + 1,)),
            dma((7,)), dma((7,)), dma((len(GROUPS) * 7,)), dma((len(GROUPS) * 7,)), dma((7,)), dma((7,)), dma((7,)), dma((7,)),
        ],
        compiler_params=pltpu.CompilerParams(
            collective_id=0, has_side_effects=True, vmem_limit_bytes=56 * 1024 * 1024
        ),
    )(jacobian, misfit.reshape(16, 128), taps.reshape(1, ORDER))
    fisher, newton = pl.pallas_call(
        outputs,
        out_shape=(jax.ShapeDtypeStruct((8, WIDTH), F32), jax.ShapeDtypeStruct((1, 8), F32)),
        in_specs=[vmem],
        out_specs=(vmem, vmem),
    )(pltpu.with_memory_space_constraint(rows, pltpu.VMEM))
    return fisher, newton.reshape(8)


def solution(mesh):
    in_specs = (P(("net", "tm"), None), P(("net", "tm")), P("net"))
    out_specs = (P(("net", "tm"), None), P(("net", "tm")))
    return jax.shard_map(shards, mesh=mesh, in_specs=in_specs, out_specs=out_specs, check_vma=False)
```

```python
import jax
import jax.numpy as jnp
from jax import lax
from jax.experimental import pallas as pl
from jax.experimental.pallas import tpu as pltpu
from jax.sharding import PartitionSpec as P

NX, NZ, NY, NC = 4, 8, 2, 2
NU = NX * NY
OWNERS = NX * NZ * NY * NC
MESH = pl.DeviceIdType.MESH
BF16, F32 = jnp.bfloat16, jnp.float32

ROWS, WIDTH, ORDER = 2048, 1024, 64
BLOCK = 192
GREET = 8
BOUNDS = [0, 512, 1024, 1536, 2048]
CHUNKS = len(BOUNDS) - 1
KROWS = 256
MROWS = 256
ACOLS = 256
BCOLS = WIDTH - ACOLS
AHALF, BHALF = ACOLS // 2, BCOLS // 2
TOTAL = ROWS * OWNERS
XY_STEPS = [(0, 1), (2, 1), (1, 1), (3, 1), (2, 0), (1, 0), (3, 0)]
Z_STEPS = [4, 3, 5, 2, 6, 1, 7]
GROUPS = [(0, 4), (4, 8)]
PLAN = [("gram", "a"), ("send", 0), ("send", "a"), ("gram", 1), ("send", 1)]
PASSES = ["a", 0, 1]


def position(x, z, y, c):
    return ((lax.rem(x, NX) * NZ + lax.rem(z, NZ)) * NY + lax.rem(y, NY)) * NC + lax.rem(c, NC)


def folded(rows):
    half = rows.shape[1] // 2
    return jnp.concatenate([rows[:, :half], rows[:, half:]], axis=0)


def unfolded(piece):
    return jnp.concatenate([piece[:8], piece[8:]], axis=1)


def place_of(step):
    return (step - 2) % NZ


def beside(shape, base):
    r = lax.broadcasted_iota(jnp.int32, shape, 0)
    lane = lax.broadcasted_iota(jnp.int32, shape, 1) - base
    return lane == lax.rem(r + 1, 8), lane == lax.rem(r + 2, 8)


def two_terms(value):
    high = value.astype(BF16).astype(F32)
    return high, value - high


def place(rows, base, grad):
    one, two = beside(rows.shape, base)
    high, low = two_terms(grad)
    return jnp.where(one, high, jnp.where(two, low, rows))


def split_again(rows, base):
    one, two = beside(rows.shape, base)
    high, low = two_terms(jnp.sum(jnp.where(one | two, rows, 0.0), axis=0, keepdims=True))
    return jnp.where(one, high, jnp.where(two, low, rows))


def in_tiles(rows, first, change):
    if first < 0 or first * 128 >= rows.shape[1]:
        return rows
    low, high = first * 128, first * 128 + 256
    parts = [rows[:, :low], change(rows[:, low:high]), rows[:, high:]]
    return jnp.concatenate([part for part in parts if part.shape[1]], axis=1)


def kernel(
    jac, mis_in, taps_in, rows_out,
    mis, taps, xbuf, white, white_t, wm_rows, mis_tail, acc,
    keep_a, keep_b, core_sa, core_sb, core_ra, core_rb,
    s1a, s1b, r1a, r1b, a2, b2, s2a, s2b, r2a, r2b,
    load_sem, halo_ss, halo_rs, core_ss, core_rs,
    s1a_ss, s1a_rs, s1b_ss, s1b_rs, s2a_ss, s2a_rs, s2b_ss, s2b_rs,
):
    me = lax.axis_index("tm")
    x, z, y, c = me // (NZ * NY * NC), (me // (NY * NC)) % NZ, (me // NC) % NY, me % NC
    sibling = position(x, z, y, c + 1)
    after, before = lax.rem(me + 1, OWNERS), lax.rem(me + OWNERS - 1, OWNERS)
    xy_dev = [position(x + dx, z, y + dy, c) for dx, dy in XY_STEPS]
    xy_own = [lax.rem(x + dx, NX) * NY + lax.rem(y + dy, NY) for dx, dy in XY_STEPS]
    z_dev = [position(x, z + dz, y, c) for dz in Z_STEPS]
    z_own = [lax.rem(z + dz, NZ) for dz in Z_STEPS]
    u = x * NY + y
    z_at = [lax.rem(z + 2 + p, NZ) for p in range(NZ)]

    loads = []
    for i, (low, high) in enumerate(zip(BOUNDS[:-1], BOUNDS[1:])):
        loads.append(pltpu.make_async_copy(
            jac.at[pl.ds(low, high - low)], xbuf.at[pl.ds(ORDER + low, high - low)], load_sem.at[i]
        ))

    small = [
        pltpu.make_async_copy(taps_in, taps, load_sem.at[CHUNKS]),
        pltpu.make_async_copy(mis_in, mis, load_sem.at[CHUNKS + 1]),
    ]
    for load in small + loads[::-1]:
        load.start()

    barrier = pltpu.get_barrier_semaphore()
    partners = [sibling, after, before] + xy_dev + z_dev
    for device in partners:
        pl.semaphore_signal(barrier, inc=1, device_id={"tm": device}, device_id_type=MESH)

    for load in small:
        load.wait()

    coef = jnp.broadcast_to(taps[...].astype(BF16), (16, ORDER))
    lag_of = lax.broadcasted_iota(jnp.int32, (ORDER, 256), 0)
    lane_of = lax.broadcasted_iota(jnp.int32, (ORDER, 256), 1)
    flip = (lag_of + lane_of == ORDER - 1).astype(F32).astype(BF16)
    first = jnp.dot(coef, flip, preferred_element_type=F32)[:1]
    lane = lax.broadcasted_iota(jnp.int32, (1, 256), 1)
    first = jnp.where(lane == ORDER, 1.0, -first)
    matrix = pltpu.roll(jnp.broadcast_to(first, (BLOCK, 256)), 0, 1, stride=1, stride_axis=0).astype(BF16)
    mis_matrix = pltpu.roll(jnp.broadcast_to(first, (128, 256)), ORDER, 1, stride=1, stride_axis=0).astype(BF16)

    def whiten_misfit(tail):
        here = mis[...].astype(F32)
        row_of = lax.broadcasted_iota(jnp.int32, (16, 128), 0)
        previous = jnp.where(row_of == 0, pltpu.roll(tail, 1, 0), pltpu.roll(here, 1, 0))
        both = jnp.concatenate([previous, here], axis=1).astype(BF16)
        return lax.dot_general(both, mis_matrix, (((1,), (1,)), ((), ())), preferred_element_type=F32)

    def put_misfit(white_mis, i):
        wm_rows[:, i * 128 : (i + 1) * 128] = jnp.broadcast_to(white_mis[i : i + 1], (16, 128)).astype(BF16)

    white_mis = whiten_misfit(jnp.zeros((16, 128), F32))
    for i in range(1, 16):
        put_misfit(white_mis, i)

    def whiten(start, rows):
        out = jnp.dot(
            matrix[:rows, : rows + ORDER], xbuf[start : start + rows + ORDER], preferred_element_type=F32
        )
        white[start : start + rows] = out.astype(BF16)

    def transpose(i):
        block = white[i * KROWS : (i + 1) * KROWS].T
        for zo in range(NZ):
            for xo in range(NX):
                pass
        white_t[:, i * KROWS : (i + 1) * KROWS] = block

    halo = pltpu.make_async_remote_copy(
        src_ref=jac.at[pl.ds(ROWS - ORDER, ORDER)], dst_ref=xbuf.at[pl.ds(0, ORDER)],
        send_sem=halo_ss.at[0], recv_sem=halo_rs.at[0], device_id={"tm": after}, device_id_type=MESH,
    )
    mis_halo = pltpu.make_async_remote_copy(
        src_ref=mis_in, dst_ref=mis_tail,
        send_sem=halo_ss.at[1], recv_sem=halo_rs.at[1], device_id={"tm": after}, device_id_type=MESH,
    )

    ready, turned = CHUNKS, ROWS // KROWS
    for start in list(range(0, ROWS, BLOCK))[:0:-1]:
        rows = min(BLOCK, ROWS - start)
        while BOUNDS[ready] > start - ORDER:
            ready -= 1
            loads[ready].wait()
        if start == GREET * BLOCK:
            pl.semaphore_wait(barrier, len(partners))

            @pl.when(me < OWNERS - 1)
            def _():
                halo.start()
                mis_halo.start()

        whiten(start, rows)
        while (turned - 1) * KROWS >= start:
            turned -= 1
            transpose(turned)
    while ready > 0:
        ready -= 1
        loads[ready].wait()

    def z_group(low, high, row):
        xo, p = row // ((high - low) * 32), low + row // 32 % (high - low)
        return pl.ds(pl.multiple_of(xo * 256 + z_at[p] * 32, 32), 32)

    def product(group, left, right, first, last):
        low, high = group
        rows, parts = NX * (high - low) * 32, []
        for i in range(0, rows, MROWS):
            lhs = [white_t[z_group(low, high, j), first:last] for j in range(i, i + MROWS, 32)]
            if i + MROWS == rows:
                lhs.append(wm_rows[:, first:last])
            lhs = jnp.concatenate(lhs, axis=0)
            parts.append(jnp.dot(lhs, white[first:last, left:right], preferred_element_type=F32))
        return jnp.concatenate(parts, axis=0)

    def gram_a(first, last):
        return product((0, NZ), 0, ACOLS, first, last)

    def gram_b(g, first, last):
        return product(GROUPS[g], ACOLS, WIDTH, first, last)

    acc[...] = gram_b(0, KROWS, ROWS)

    @pl.when(me > 0)
    def _():
        halo.wait_recv()
        mis_halo.wait_recv()

    @pl.when(me == 0)
    def _():
        xbuf[:ORDER] = jnp.zeros((ORDER, WIDTH), BF16)
        mis_tail[...] = jnp.zeros_like(mis_tail)

    whiten(0, BLOCK)
    transpose(0)
    put_misfit(whiten_misfit(mis_tail[...].astype(F32)), 0)

    def to_sibling(src, dst, k):
        return pltpu.make_async_remote_copy(
            src_ref=src, dst_ref=dst, send_sem=core_ss.at[k], recv_sem=core_rs.at[k],
            device_id={"tm": sibling}, device_id_type=MESH,
        )

    mine_first = c == 0

    def base_of(p, yo, side):
        return z_at[p] * 32 + (yo * NC + side) * 8

    def deal(rows, grad, first, p, yo, keep, send, index):
        pair = []
        for side in range(NC):
            part = rows[side * 8 : side * 8 + 8]

            def change(tiles, side=side):
                return place(tiles, base_of(p, yo, side), grad[:, first * 128 : first * 128 + 256])

            pair.append(folded(in_tiles(part, first, change)))
        keep[index] = jnp.where(mine_first, pair[0], pair[1])
        send[index] = jnp.where(mine_first, pair[1], pair[0]).astype(BF16)

    def both_cores(keep, received, index, first, p, yo):
        rows = keep[index] + received[index].astype(F32)
        if first < 0 or first * 128 >= 2 * rows.shape[1]:
            return rows.astype(BF16)
        rows = in_tiles(unfolded(rows), first, lambda tiles: split_again(tiles, base_of(p, yo, c)))
        return folded(rows).astype(BF16)

    stage1a, stage1b, stage2a, stage2b, core = [], {}, [], {}, {}

    def slot(g, own, p):
        low, high = GROUPS[g]
        return low * NU + own * (high - low) + p - low

    def finish_b(g, out):
        low, high = GROUPS[g]
        row = 0
        for xo in range(NX):
            for p in range(low, high):
                for yo in range(NY):
                    deal(
                        out[row : row + 16], out[-16:-15], xo * 2 - 2, p, yo,
                        keep_b, core_sb, slot(g, xo * NY + yo, p),
                    )
                    row += 16
        span = pl.ds(low * NU, (high - low) * NU)
        core[g] = to_sibling(core_sb.at[span], core_rb.at[span], 1 + g)
        core[g].start()

    def send_b(g):
        low, high = GROUPS[g]
        core[g].wait_recv()
        for xo in range(NX):
            for yo in range(NY):
                for p in range(low, high):
                    index = slot(g, xo * NY + yo, p)
                    s1b[index] = both_cores(keep_b, core_rb, index, xo * 2 - 2, p, yo)
        for k, (device, own) in enumerate(zip(xy_dev, xy_own)):
            copy = pltpu.make_async_remote_copy(
                src_ref=s1b.at[pl.ds(slot(g, own, low), high - low)], dst_ref=r1b.at[k, low:high],
                send_sem=s1b_ss.at[g * 7 + k], recv_sem=s1b_rs.at[g * 7 + k],
                device_id={"tm": device}, device_id_type=MESH,
            )
            copy.start()
            stage1b[g, k] = copy

    def finish_a(out):
        row = 0
        for xo in range(NX):
            for p in range(NZ):
                for yo in range(NY):
                    deal(
                        out[row : row + 16], out[WIDTH : WIDTH + 1], xo * 2, p, yo,
                        keep_a, core_sa, p * NU + xo * NY + yo,
                    )
                    row += 16
        core["a"] = to_sibling(core_sa, core_ra, 0)
        core["a"].start()

    def send_a():
        core["a"].wait_recv()
        for p in range(NZ):
            for xo in range(NX):
                for yo in range(NY):
                    index = p * NU + xo * NY + yo
                    s1a[index] = both_cores(keep_a, core_ra, index, xo * 2, p, yo)
        for k, (device, step) in enumerate(zip(z_dev, Z_STEPS)):
            copy = pltpu.make_async_remote_copy(
                src_ref=s1a.at[pl.ds(place_of(step) * NU, NU)], dst_ref=r1a.at[k],
                send_sem=s1a_ss.at[k], recv_sem=s1a_rs.at[k], device_id={"tm": device}, device_id_type=MESH,
            )
            copy.start()
            stage1a.append(copy)

    def send(item):
        if item == "a":
            send_a()
        else:
            send_b(item)

    finish_b(0, acc[...] + gram_b(0, 0, KROWS))
    for act, item in PLAN:
        if act == "send":
            send(item)
        elif item == "a":
            finish_a(gram_a(0, ROWS))
        else:
            finish_b(item, gram_b(item, 0, ROWS))

    def pass_b(g):
        low, high = GROUPS[g]
        span = pl.ds(slot(g, u, low), high - low)
        b2[low:high] = keep_b[span] + core_rb[span].astype(F32)
        for k in range(7):
            stage1b[g, k].wait_recv()
            b2[low:high] += r1b[k, low:high].astype(F32)
        for p in range(low, high):
            lane = x * 256 - ACOLS + base_of(p, y, c)
            s2b[p] = folded(split_again(unfolded(b2[p]), lane)).astype(BF16)
        for k, (device, step) in enumerate(zip(z_dev, Z_STEPS)):
            p = place_of(step)
            if low <= p < high:
                copy = pltpu.make_async_remote_copy(
                    src_ref=s2b.at[p], dst_ref=r2b.at[k],
                    send_sem=s2b_ss.at[k], recv_sem=s2b_rs.at[k], device_id={"tm": device}, device_id_type=MESH,
                )
                copy.start()
                stage2b[k] = copy

    def pass_a():
        span = pl.ds(place_of(0) * NU, NU)
        a2[...] = keep_a[span] + core_ra[span].astype(F32)
        for k, copy in enumerate(stage1a):
            copy.wait_recv()
            a2[...] += r1a[k].astype(F32)
        for xo in range(NX):
            for yo in range(NY):
                rows = a2[xo * NY + yo]
                if xo == 0:
                    rows = folded(split_again(unfolded(rows), base_of(place_of(0), yo, c)))
                s2a[xo * NY + yo] = rows.astype(BF16)
        for k, (device, own) in enumerate(zip(xy_dev, xy_own)):
            copy = pltpu.make_async_remote_copy(
                src_ref=s2a.at[own], dst_ref=r2a.at[k],
                send_sem=s2a_ss.at[k], recv_sem=s2a_rs.at[k], device_id={"tm": device}, device_id_type=MESH,
            )
            copy.start()
            stage2a.append(copy)

    for item in PASSES:
        if item == "a":
            pass_a()
        else:
            pass_b(item)

    last_a, last_b = a2[u], b2[place_of(0)]
    for k, copy in enumerate(stage2a):
        copy.wait_recv()
        last_a = last_a + r2a[k].astype(F32)

    @pl.when(me < OWNERS - 1)
    def _():
        halo.wait_send()
        mis_halo.wait_send()

    for copy in list(core.values()) + stage1a + list(stage1b.values()) + stage2a:
        copy.wait_send()

    for k, copy in stage2b.items():
        copy.wait_recv()
        last_b = last_b + r2b[k].astype(F32)
    rows_out[:, :ACOLS] = unfolded(last_a)
    rows_out[:, ACOLS:] = unfolded(last_b)

    for copy in stage2b.values():
        copy.wait_send()


def outputs(rows_ref, fisher, newton):
    rows = rows_ref[...]
    r = lax.broadcasted_iota(jnp.int32, rows.shape, 0)
    col = lax.broadcasted_iota(jnp.int32, rows.shape, 1) - lax.axis_index("tm") * 8
    one, two, on = col == lax.rem(r + 1, 8), col == lax.rem(r + 2, 8), col == r

    def picked(mask, values):
        return jnp.broadcast_to(jnp.sum(jnp.where(mask, values, 0.0), axis=1, keepdims=True), (8, 128))

    grad = pltpu.roll(picked(one, rows), 1, 0) + pltpu.roll(picked(two, rows), 2, 0)
    diagonal = picked(on, rows)
    mirror_one = picked(on, pltpu.roll(rows, 7, 0))[:, :1]
    mirror_two = picked(on, pltpu.roll(rows, 6, 0))[:, :1]
    fisher[...] = jnp.where(one, mirror_one, jnp.where(two, mirror_two, rows)) * (1.0 / TOTAL)
    r8 = lax.broadcasted_iota(jnp.int32, (8, 128), 0)
    c8 = lax.broadcasted_iota(jnp.int32, (8, 128), 1)
    newton[...] = jnp.sum(jnp.where(r8 == c8, grad / diagonal, 0.0), axis=0, keepdims=True)[:, :8]


def shards(jacobian, misfit, taps):
    dma = pltpu.SemaphoreType.DMA
    vmem = pl.BlockSpec(memory_space=pltpu.VMEM)
    rows = pl.pallas_call(
        kernel,
        out_shape=pltpu.VMEM((8, WIDTH), F32),
        in_specs=[pl.BlockSpec(memory_space=pl.ANY)] * 3,
        out_specs=vmem,
        scratch_shapes=[
            pltpu.VMEM((16, 128), BF16),
            pltpu.VMEM((1, ORDER), F32),
            pltpu.VMEM((ROWS + ORDER, WIDTH), BF16),
            pltpu.VMEM((ROWS, WIDTH), BF16),
            pltpu.VMEM((WIDTH, ROWS), BF16),
            pltpu.VMEM((16, ROWS), BF16),
            pltpu.VMEM((16, 128), BF16),
            pltpu.VMEM((NX * (GROUPS[0][1] - GROUPS[0][0]) * 32 + 16, BCOLS), F32),
            pltpu.VMEM((64, 16, AHALF), F32),
            pltpu.VMEM((64, 16, BHALF), F32),
            pltpu.VMEM((64, 16, AHALF), BF16),
            pltpu.VMEM((64, 16, BHALF), BF16),
            pltpu.VMEM((64, 16, AHALF), BF16),
            pltpu.VMEM((64, 16, BHALF), BF16),
            pltpu.VMEM((64, 16, AHALF), BF16),
            pltpu.VMEM((64, 16, BHALF), BF16),
            pltpu.VMEM((7, 8, 16, AHALF), BF16),
            pltpu.VMEM((7, NZ, 16, BHALF), BF16),
            pltpu.VMEM((8, 16, AHALF), F32),
            pltpu.VMEM((NZ, 16, BHALF), F32),
            pltpu.VMEM((8, 16, AHALF), BF16),
            pltpu.VMEM((8, 16, BHALF), BF16),
            pltpu.VMEM((7, 16, AHALF), BF16),
            pltpu.VMEM((7, 16, BHALF), BF16),
            dma((CHUNKS + 2,)), dma((2,)), dma((2,)), dma((len(GROUPS) + 1,)), dma((len(GROUPS) + 1,)),
            dma((7,)), dma((7,)), dma((len(GROUPS) * 7,)), dma((len(GROUPS) * 7,)), dma((7,)), dma((7,)), dma((7,)), dma((7,)),
        ],
        compiler_params=pltpu.CompilerParams(
            collective_id=0, has_side_effects=True, vmem_limit_bytes=56 * 1024 * 1024
        ),
    )(jacobian, misfit.reshape(16, 128), taps.reshape(1, ORDER))
    fisher, newton = pl.pallas_call(
        outputs,
        out_shape=(jax.ShapeDtypeStruct((8, WIDTH), F32), jax.ShapeDtypeStruct((1, 8), F32)),
        in_specs=[vmem],
        out_specs=(vmem, vmem),
    )(pltpu.with_memory_space_constraint(rows, pltpu.VMEM))
    return fisher, newton.reshape(8)


def solution(mesh):
    in_specs = (P(("net", "tm"), None), P(("net", "tm")), P("net"))
    out_specs = (P(("net", "tm"), None), P(("net", "tm")))
    return jax.shard_map(shards, mesh=mesh, in_specs=in_specs, out_specs=out_specs, check_vma=False)
```
